512 devices in a mesh: dp: 32 (over z, x), tensor: 16 (over y, core).
Axes of the slice: x: 4, y: 8, z: 8, core: 2. Of those that a mesh axis runs over, the one named last changes fastest.
Arguments:
- tokens: bfloat16 [16384, 8192], P('dp', 'tensor'), may hold values from -6 to 6
- key_value_weight: bfloat16 [8192, 2048], P('tensor'), may hold values from -0.0625 to 0.0625
- adapter_down_weight: bfloat16 [96, 64, 8192], P('dp', None, 'tensor'), may hold values from -0.0625 to 0.0625
- adapter_up_weight: bfloat16 [96, 64, 2048], P('dp', None, 'tensor'), may hold values from -0.75 to 0.75
- cotangent: bfloat16 [16384, 2048], P('dp', 'tensor'), may hold values from -3 to 3
- sequence_adapter_index: int32 [512], replicated, may hold values from 0 to 95, as said below
- adapter_storage_row: int32 [96], replicated, may hold values from 0 to 95, as said below
Outputs:
- key_value_output: bfloat16 [16384, 2048], P('dp', 'tensor')
- token_gradient: bfloat16 [16384, 8192], P('dp', 'tensor')
- grad_down: float32 [96, 64, 8192], P('dp', None, 'tensor')
- grad_up: float32 [96, 64, 2048], P('dp', None, 'tensor')
The draws below stay inside these ranges and needn't reach their ends.
Inputs may be any that keep to these rules, and one draw needn't show every extreme that they name: Each value appears once: adapter a is held at row adapter_storage_row[a] of adapter_down_weight, adapter_up_weight, grad_down and grad_up, on index adapter_storage_row[a] // 3 of dp. `sequence_adapter_index`: the 16 sequences i that share one value of i // 16 use adapters held on 16 different indices of dp.
All inputs are finite; a program needn't handle non-finite values.
Results may differ from the reference program's by a relative error of at most 0.02.
Values may be sent and summed in bfloat16 or wider, within the bound.
No kernel may reach another device: no remote copies, remote signals or barrier semaphores. Data moves between devices by JAX's collectives and lax.ppermute only.
A program may use at most 64 MiB of HBM per device.

```python
import jax
import jax.numpy as jnp
from jax import lax

MODEL_WIDTH = 8192
ADAPTER_RANK = 64
SEQS_DEV = 16
ADP_DEV = 3
KEY_VALUE_WIDTH = 2048
TOKENS = 16384
ADAPTER_TOTAL = 96
N_DP = 32
N_TENSOR = 16


def adapter_tables(key):
    base_key = jax.random.fold_in(key, 11)
    storage = jax.random.permutation(jax.random.fold_in(base_key, 1), ADP_DEV * N_DP).astype(jnp.int32)
    reader_keys = jax.random.split(jax.random.fold_in(base_key, 2), N_DP)

    def owners_for(reader_key):
        return jax.random.permutation(reader_key, N_DP)[:SEQS_DEV]
    owners = jax.vmap(owners_for)(reader_keys).astype(jnp.int32)
    draw_one = jax.random.randint(jax.random.fold_in(base_key, 3), (N_DP, SEQS_DEV), 0, ADP_DEV)
    draw_two = jax.random.randint(jax.random.fold_in(base_key, 4), (N_DP, SEQS_DEV), 0, ADP_DEV)
    within = jnp.minimum(draw_one, draw_two).astype(jnp.int32)
    held_rows = (owners * ADP_DEV + within).reshape(-1)
    inverse = jnp.argsort(storage).astype(jnp.int32)
    chosen = inverse[held_rows]
    return (storage, chosen.astype(jnp.int32))


def draw_adapter_storage_row(key, part):
    return adapter_tables(key)[0]


def draw_sequence_adapter_index(key, part):
    return adapter_tables(key)[1]


def block_levels(stream_key, shape, cuts, low, top_value):
    factor_of = 1.0
    for axis_at, shards_of in cuts:
        draws = jax.random.uniform(jax.random.fold_in(jax.random.fold_in(stream_key, 6), axis_at), (shards_of,), jnp.float32, low / len(cuts), top_value / len(cuts))
        factor_of = factor_of * jnp.repeat(jnp.exp(draws), shape[axis_at] // shards_of).reshape((-1,) + (1,) * (len(shape) - 1 - axis_at))
    return factor_of


def scatter_about(rng, dims, deviation, bound, cuts=(), held_as=jnp.bfloat16):
    factor_of = block_levels(rng, dims, cuts, -0.22, 0.18) if cuts else 1.0
    array = jax.random.normal(rng, dims, jnp.float32) * deviation * factor_of
    return jnp.minimum(jnp.maximum(array, -bound), bound).astype(held_as)


def setup_inputs(seed: int = 0) -> dict:
    keys = jax.random.split(jax.random.key(seed), 8)
    return {
        "tokens": scatter_about(keys[0], (TOKENS, MODEL_WIDTH), 1.0, 6.0, ((0, 32), (1, 16))),
        "key_value_weight": scatter_about(keys[1], (MODEL_WIDTH, KEY_VALUE_WIDTH), MODEL_WIDTH ** -0.5, 0.0625, ((0, 16),)),
        "adapter_down_weight": scatter_about(keys[2], (ADAPTER_TOTAL, ADAPTER_RANK, MODEL_WIDTH), MODEL_WIDTH ** -0.5, 0.0625, ((0, 32), (2, 16))),
        "adapter_up_weight": scatter_about(keys[3], (ADAPTER_TOTAL, ADAPTER_RANK, KEY_VALUE_WIDTH), ADAPTER_RANK ** -0.5, 0.75, ((0, 32), (2, 16))),
        "cotangent": scatter_about(keys[4], (TOKENS, KEY_VALUE_WIDTH), 0.5, 3.0, ((0, 32), (1, 16))),
        "sequence_adapter_index": draw_sequence_adapter_index(jax.random.fold_in(keys[7], 71), 0),
        "adapter_storage_row": draw_adapter_storage_row(jax.random.fold_in(keys[7], 71), 0),
    }


adapter_scale = 0.25


def reference(tokens, key_value_weight, adapter_down_weight, adapter_up_weight, cotangent, sequence_adapter_index, adapter_storage_row):
    adapters = adapter_storage_row.shape[0]
    seq_total = sequence_adapter_index.shape[0]
    adapter_codes = jnp.arange(adapters, dtype=jnp.int32)
    matches = sequence_adapter_index[:, None] == adapter_codes[None, :]
    seq_rows = jnp.sum(jnp.where(matches, adapter_storage_row[None, :], 0), axis=1).astype(jnp.int32)
    row_hits = seq_rows[:, None] == adapter_codes[None, :]
    usage_count = jnp.sum(row_hits.astype(jnp.float32), axis=0)
    inverse_use = 1.0 / jnp.maximum(usage_count, 1.0)
    feature_width = tokens.shape[1]
    seq_length = tokens.shape[0] // seq_total
    block_span = feature_width // N_TENSOR
    out_width = key_value_weight.shape[1]
    weight_blocks = key_value_weight.reshape(N_TENSOR, block_span, out_width).astype(jnp.float32)
    weight_turned = key_value_weight.T
    token_sequences = tokens.reshape(seq_total, seq_length, feature_width)
    cot_seqs = cotangent.reshape(seq_total, seq_length, out_width)

    def one_sequence(totals, inputs):
        grad_down, grad_up = totals
        sequence_tokens, sequence_cotangent, sequence_row = inputs
        down_matrix_rows = lax.dynamic_index_in_dim(adapter_down_weight, sequence_row, 0, keepdims=False)
        up_matrix_rows = lax.dynamic_index_in_dim(adapter_up_weight, sequence_row, 0, keepdims=False)
        pieces = sequence_tokens.reshape(seq_length, N_TENSOR, block_span).astype(jnp.float32)
        partial_value = jnp.einsum("lnd,ndo->nlo", pieces, weight_blocks)
        partial_round = lax.optimization_barrier(partial_value.astype(jnp.bfloat16)).astype(jnp.float32)
        frozen_backbone = jnp.sum(partial_round, axis=0)
        inner_full = jnp.dot(sequence_tokens, down_matrix_rows.T, preferred_element_type=jnp.float32)
        middle_round = inner_full.astype(jnp.bfloat16)
        back_full = jnp.dot(sequence_cotangent, up_matrix_rows.T, preferred_element_type=jnp.float32)
        backward_round = back_full.astype(jnp.bfloat16)
        output_list = (frozen_backbone + adapter_scale * jnp.dot(middle_round, up_matrix_rows, preferred_element_type=jnp.float32)).astype(jnp.bfloat16)
        grad_in = (jnp.dot(sequence_cotangent, weight_turned, preferred_element_type=jnp.float32)
                   + adapter_scale * jnp.dot(backward_round, down_matrix_rows, preferred_element_type=jnp.float32)).astype(jnp.bfloat16)
        down_term = (adapter_scale * jnp.dot(backward_round.T, sequence_tokens, preferred_element_type=jnp.float32)).astype(jnp.bfloat16)
        up_term = (adapter_scale * jnp.dot(middle_round.T, sequence_cotangent, preferred_element_type=jnp.float32)).astype(jnp.bfloat16)
        grad_down = grad_down.at[sequence_row].add(down_term.astype(jnp.float32))
        grad_up = grad_up.at[sequence_row].add(up_term.astype(jnp.float32))
        return (grad_down, grad_up), (output_list, grad_in)

    down_start_offset = jnp.zeros(adapter_down_weight.shape, jnp.float32)
    up_start_offset = jnp.zeros(adapter_up_weight.shape, jnp.float32)
    (grad_down, grad_up), (output_list, grad_in) = lax.scan(one_sequence, (down_start_offset, up_start_offset), (token_sequences, cot_seqs, seq_rows))
    key_value_output = output_list.reshape(seq_total * seq_length, out_width)
    token_gradient = grad_in.reshape(seq_total * seq_length, feature_width)
    grad_down = grad_down * inverse_use[:, None, None]
    grad_up = grad_up * inverse_use[:, None, None]
    return (key_value_output, token_gradient, grad_down, grad_up)
```

```python
import functools

import jax
import jax.numpy as jnp
from jax import lax
from jax.experimental import pallas as pl
from jax.experimental.pallas import tpu as pltpu
from jax.sharding import PartitionSpec as P

adapter_scale = 0.25
f32 = jnp.float32
bf16 = jnp.bfloat16
SMEM = pl.BlockSpec(memory_space=pltpu.SMEM)
VMEM = pl.BlockSpec(memory_space=pltpu.VMEM)
VMEM_LIMIT = 40 * 1024 * 1024


def local_call(body, out_shape, specs, scratch=(), flops=0, moved=0):
    multiple = isinstance(out_shape, (tuple, list))
    return pl.pallas_call(
        body,
        out_shape=out_shape,
        in_specs=specs,
        out_specs=(VMEM,) * len(out_shape) if multiple else VMEM,
        scratch_shapes=list(scratch),
        compiler_params=pltpu.CompilerParams(vmem_limit_bytes=VMEM_LIMIT),
        cost_estimate=pl.CostEstimate(flops=flops, bytes_accessed=moved, transcendentals=0),
    )


def owner_of(first, index_ref, storage_ref, held, j):
    return storage_ref[index_ref[first + j]] // held


def spread_body(held, first_ref, index_ref, storage_ref, rows_ref, out_ref):
    slots, length, width = out_ref.shape
    out_ref[...] = jnp.zeros_like(out_ref)
    first = first_ref[0]
    for j in range(rows_ref.shape[0] // length):
        owner = owner_of(first, index_ref, storage_ref, held, j)
        out_ref[owner] = rows_ref[j * length : (j + 1) * length, :]


def projection_body(core_ref, tokens_ref, weight_ref, own_ref, send_ref):
    blocks, rows, width = own_ref.shape
    core = core_ref[0]
    tokens = tokens_ref[...]
    for b in range(blocks):
        part = jnp.dot(
            tokens,
            weight_ref[:, b * 2 * width : (b + 1) * 2 * width],
            preferred_element_type=f32,
        ).astype(bf16)
        low, high = part[:, :width], part[:, width:]

        @pl.when(core == 0)
        def _():
            own_ref[b] = low
            send_ref[b] = high

        @pl.when(core != 0)
        def _():
            own_ref[b] = high
            send_ref[b] = low


def rank_body(pick_ref, rows_ref, adapter_ref, out_ref):
    slots, length, width = rows_ref.shape
    held, rank, _ = adapter_ref.shape
    half = slots // 2
    flat = rows_ref[...].reshape(slots * length, width)
    dims = (((1,), (1,)), ((), ()))
    totals = [
        lax.dot_general(flat, adapter_ref[a], dims, preferred_element_type=f32) for a in range(held)
    ]
    chosen = []
    for s in range(slots):
        at = slice(s * length, (s + 1) * length)
        value = jnp.zeros((length, rank), f32)
        for a in range(held):
            value = jnp.where(pick_ref[s] == a, totals[a][at], value)
        chosen.append(value)
    for s in range(half):
        out_ref[s * length : (s + 1) * length, :] = jnp.concatenate(
            [chosen[s], chosen[s + half]], axis=1
        ).astype(bf16)


def fill_masked(pick_ref, pairs_ref, masked_ref, slots, length, held, rank):
    half = slots // 2
    for s in range(slots):
        left = (s // half) * rank
        block = pairs_ref[(s % half) * length : (s % half + 1) * length, :][:, left : left + rank]
        for a in range(held):
            masked_ref[s * length : (s + 1) * length, a * rank : (a + 1) * rank] = jnp.where(
                pick_ref[s] == a, block, jnp.zeros_like(block)
            )


def expand_body(pick_ref, pairs_ref, adapter_ref, out_ref, masked_ref):
    slots, length, width = out_ref.shape
    held, rank, _ = adapter_ref.shape
    fill_masked(pick_ref, pairs_ref, masked_ref, slots, length, held, rank)
    stacked = adapter_ref[...].reshape(held * rank, width)
    value = jnp.dot(masked_ref[...], stacked, preferred_element_type=f32) * adapter_scale
    out_ref[...] = value.astype(bf16).reshape(slots, length, width)


def gradient_body(pick_ref, scale_ref, pairs_ref, rows_ref, out_ref, masked_ref):
    slots, length, width = rows_ref.shape
    held, rank, _ = out_ref.shape
    fill_masked(pick_ref, pairs_ref, masked_ref, slots, length, held, rank)
    total = lax.dot_general(
        masked_ref[...],
        rows_ref[...].reshape(slots * length, width),
        (((0,), (0,)), ((), ())),
        preferred_element_type=f32,
    )
    for a in range(held):
        out_ref[a] = total[a * rank : (a + 1) * rank] * scale_ref[a]


def input_gradient_body(
    held, first_ref, index_ref, storage_ref, cot_ref, weight_ref, came_ref, out_ref, total_ref
):
    blocks, rows, width = cot_ref.shape
    length = came_ref.shape[1]
    dims = (((1,), (1,)), ((), ()))
    for b in range(blocks // 2):
        pair = jnp.concatenate([cot_ref[2 * b], cot_ref[2 * b + 1]], axis=1)
        part = lax.dot_general(
            pair,
            weight_ref[:, 2 * b * width : 2 * (b + 1) * width],
            dims,
            preferred_element_type=f32,
        )
        total_ref[...] = part if b == 0 else total_ref[...] + part
    first = first_ref[0]
    for j in range(rows // length):
        owner = owner_of(first, index_ref, storage_ref, held, j)
        at = slice(j * length, (j + 1) * length)
        out_ref[at, :] = (total_ref[at, :] + came_ref[owner].astype(f32)).astype(bf16)


def output_body(held, first_ref, index_ref, storage_ref, base_ref, came_ref, out_ref):
    length = came_ref.shape[1]
    first = first_ref[0]
    for j in range(base_ref.shape[0] // length):
        owner = owner_of(first, index_ref, storage_ref, held, j)
        at = slice(j * length, (j + 1) * length)
        out_ref[at, :] = (base_ref[at, :].astype(f32) + came_ref[owner].astype(f32)).astype(bf16)


def rank_total(part, count):
    cores = [[t, t + 1] for t in range(0, count, 2)]
    half = part.shape[0] // 2
    core = lax.axis_index("tensor") % 2
    both = lax.all_gather(part, "tensor", axis_index_groups=cores)
    mine = lax.dynamic_slice_in_dim(both, core * half, half, axis=1)
    total = mine.astype(f32).sum(0).astype(bf16)
    step = 2
    while step < count:
        other = lax.ppermute(total, "tensor", [(t, t ^ step) for t in range(count)])
        total = (total.astype(f32) + other.astype(f32)).astype(bf16)
        step *= 2
    return lax.all_gather(total, "tensor", axis_index_groups=cores).reshape(part.shape)


def exchange(value):
    return lax.all_to_all(value, "dp", split_axis=0, concat_axis=0, tiled=True)


def after(value, earlier):
    return lax.optimization_barrier((value, earlier))[0]


def on_device(tokens, weight, down, up, cotangent, sequence_index, storage_row):
    dp_count = lax.axis_size("dp")
    tensor_count = lax.axis_size("tensor")
    me = lax.axis_index("dp")
    held, rank, block = down.shape
    out_block = up.shape[2]
    rows = tokens.shape[0]
    seqs = sequence_index.shape[0] // dp_count
    length = rows // seqs
    slots = dp_count
    first = jnp.reshape(me * seqs, (1,)).astype(jnp.int32)
    core = jnp.reshape(lax.axis_index("tensor") % 2, (1,)).astype(jnp.int32)

    def shape(*dims, dtype=bf16):
        return jax.ShapeDtypeStruct(dims, dtype)

    def spread(value):
        width = value.shape[1]
        return local_call(
            functools.partial(spread_body, held),
            shape(slots, length, width),
            [SMEM, SMEM, SMEM, VMEM],
            moved=3 * slots * length * width,
        )(first, sequence_index, storage_row, value)

    cot_slots = exchange(spread(cotangent))

    codes = jnp.arange(storage_row.shape[0], dtype=jnp.int32)
    matches = sequence_index[:, None] == codes[None, :]
    seq_rows = jnp.sum(jnp.where(matches, storage_row[None, :], 0), axis=1)
    local = jnp.where(seq_rows // held == me, seq_rows - held * me, -1)
    pick = jnp.max(local.reshape(dp_count, seqs), axis=1).astype(jnp.int32)
    usage = jnp.sum((pick[:, None] == jnp.arange(held)[None, :]).astype(f32), axis=0)
    scale = adapter_scale / jnp.maximum(usage, 1.0)

    all_cot = lax.all_gather(cotangent, "tensor")
    half_blocks = tensor_count // 2
    own, send = local_call(
        projection_body,
        (shape(half_blocks, rows, out_block), shape(half_blocks, rows, out_block)),
        [SMEM, VMEM, VMEM],
        flops=2 * rows * block * tensor_count * out_block,
        moved=2 * (rows * block + 2 * block * tensor_count * out_block),
    )(core, tokens, weight)
    came = lax.ppermute(send, "tensor", [(t, t ^ 1) for t in range(tensor_count)])
    paired = (own.astype(f32) + came.astype(f32)).astype(bf16)
    same_core = [list(range(c, tensor_count, 2)) for c in range(2)]
    backbone = lax.psum_scatter(
        paired, "tensor", scatter_dimension=0, axis_index_groups=same_core, tiled=False
    )

    token_slots = exchange(after(spread(tokens), cot_slots))

    def rank_part(value, adapter):
        width = value.shape[2]
        return local_call(
            rank_body,
            shape(slots * length // 2, 2 * rank),
            [SMEM, VMEM, VMEM],
            flops=2 * slots * length * width * held * rank,
            moved=2 * slots * length * width,
        )(pick, value, adapter)

    masked = pltpu.VMEM((slots * length, held * rank), bf16)

    def expand(pairs, adapter):
        width = adapter.shape[2]
        return local_call(
            expand_body,
            shape(slots, length, width),
            [SMEM, VMEM, VMEM],
            [masked],
            flops=2 * slots * length * width * held * rank,
            moved=2 * slots * length * width,
        )(pick, pairs, adapter)

    def gradient(pairs, value):
        width = value.shape[2]
        return local_call(
            gradient_body,
            shape(held, rank, width, dtype=f32),
            [SMEM, SMEM, VMEM, VMEM],
            [masked],
            flops=2 * slots * length * width * held * rank,
            moved=2 * slots * length * width,
        )(pick, scale, pairs, value)

    back = rank_total(rank_part(cot_slots, up), tensor_count)
    token_parts = expand(back, down)
    token_slots, token_parts = lax.optimization_barrier((token_slots, token_parts))
    token_came = exchange(token_parts)
    inner = rank_total(rank_part(token_slots, down), tensor_count)
    output_parts = expand(inner, up)
    output_came = exchange(after(output_parts, token_came))
    grad_down = gradient(back, token_slots)
    grad_up = gradient(inner, cot_slots)

    token_gradient = local_call(
        functools.partial(input_gradient_body, held),
        shape(rows, block),
        [SMEM, SMEM, SMEM, VMEM, VMEM, VMEM],
        [pltpu.VMEM((rows, block), f32)],
        flops=2 * rows * block * tensor_count * out_block,
        moved=2 * (2 * rows * tensor_count * out_block + slots * length * block),
    )(first, sequence_index, storage_row, all_cot, weight, token_came)
    key_value_output = local_call(
        functools.partial(output_body, held),
        shape(rows, out_block),
        [SMEM, SMEM, SMEM, VMEM, VMEM],
        moved=2 * (2 * rows * out_block + slots * length * out_block),
    )(first, sequence_index, storage_row, backbone, output_came)
    return (key_value_output, token_gradient, grad_down, grad_up)


def solution(mesh):
    in_specs = (
        P("dp", "tensor"),
        P("tensor", None),
        P("dp", None, "tensor"),
        P("dp", None, "tensor"),
        P("dp", "tensor"),
        P(),
        P(),
    )
    out_specs = (
        P("dp", "tensor"),
        P("dp", "tensor"),
        P("dp", None, "tensor"),
        P("dp", None, "tensor"),
    )
    return jax.shard_map(
        on_device, mesh=mesh, in_specs=in_specs, out_specs=out_specs, check_vma=False
    )
```

```python
import functools

import jax
import jax.numpy as jnp
from jax import lax
from jax.experimental import pallas as pl
from jax.experimental.pallas import tpu as pltpu
from jax.sharding import PartitionSpec as P

adapter_scale = 0.25
f32 = jnp.float32
bf16 = jnp.bfloat16
SMEM = pl.BlockSpec(memory_space=pltpu.SMEM)
VMEM = pl.BlockSpec(memory_space=pltpu.VMEM)
VMEM_LIMIT = 40 * 1024 * 1024


def local_call(body, out_shape, specs, scratch=(), flops=0, moved=0):
    multiple = isinstance(out_shape, (tuple, list))
    return pl.pallas_call(
        body,
        out_shape=out_shape,
        in_specs=specs,
        out_specs=(VMEM,) * len(out_shape) if multiple else VMEM,
        scratch_shapes=list(scratch),
        compiler_params=pltpu.CompilerParams(vmem_limit_bytes=VMEM_LIMIT),
        cost_estimate=pl.CostEstimate(flops=flops, bytes_accessed=moved, transcendentals=0),
    )


def owner_of(place_ref, index_ref, storage_ref, held, j):
    return storage_ref[index_ref[place_ref[0] + j]] // held


def spread_body(held, place_ref, index_ref, storage_ref, tokens_ref, cot_ref, out_ref):
    slots, length, width = out_ref.shape
    block = tokens_ref.shape[1]
    out_ref[...] = jnp.zeros_like(out_ref)
    for j in range(tokens_ref.shape[0] // length):
        owner = owner_of(place_ref, index_ref, storage_ref, held, j)
        at = slice(j * length, (j + 1) * length)
        out_ref[owner, :, :block] = tokens_ref[at, :]
        out_ref[owner, :, block:] = cot_ref[at, :]


def block_columns(place_ref, offset, blocks, width):
    chip = lax.rem(place_ref[2] + offset, blocks)
    return pl.ds(pl.multiple_of(chip * width, width), width)


def projection_body(place_ref, tokens_ref, weight_ref, own_ref, send_ref):
    blocks, rows, width = own_ref.shape
    core = place_ref[1]
    tokens = tokens_ref[...]
    for b in range(blocks):
        columns = block_columns(place_ref, b, blocks, 2 * width)
        part = jnp.dot(tokens, weight_ref[:, columns], preferred_element_type=f32).astype(bf16)
        low, high = part[:, :width], part[:, width:]

        @pl.when(core == 0)
        def _():
            own_ref[b] = low
            send_ref[b] = high

        @pl.when(core != 0)
        def _():
            own_ref[b] = high
            send_ref[b] = low


def pair_body(own_ref, came_ref, *out_refs):
    for b, out_ref in enumerate(out_refs):
        out_ref[...] = (own_ref[b].astype(f32) + came_ref[b].astype(f32)).astype(bf16)


def rank_body(pick_ref, rows_ref, down_ref, up_ref, out_ref):
    slots, length, width = rows_ref.shape
    held, rank, block = down_ref.shape
    flat = rows_ref[...].reshape(slots * length, width)
    dims = (((1,), (1,)), ((), ()))
    inner = [
        lax.dot_general(flat[:, :block], down_ref[a], dims, preferred_element_type=f32)
        for a in range(held)
    ]
    back = [
        lax.dot_general(flat[:, block:], up_ref[a], dims, preferred_element_type=f32)
        for a in range(held)
    ]
    joined = [jnp.concatenate([inner[a], back[a]], axis=1) for a in range(held)]
    for s in range(slots):
        at = slice(s * length, (s + 1) * length)
        value = jnp.zeros((length, 2 * rank), f32)
        for a in range(held):
            value = jnp.where(pick_ref[s] == a, joined[a][at], value)
        out_ref[at, :] = value.astype(bf16)


def total_body(parts_ref, out_ref):
    total = jnp.sum(parts_ref[...].astype(f32), axis=0).astype(bf16)
    for b in range(out_ref.shape[0]):
        out_ref[b] = total


def fill_masked(pick_ref, ranks_ref, masked_ref, left, slots, held, rank):
    length = ranks_ref.shape[0] // slots
    for s in range(slots):
        at = slice(s * length, (s + 1) * length)
        block = ranks_ref[at, :][:, left : left + rank]
        for a in range(held):
            masked_ref[at, a * rank : (a + 1) * rank] = jnp.where(
                pick_ref[s] == a, block, jnp.zeros_like(block)
            )


def expand_body(pick_ref, ranks_ref, down_ref, up_ref, out_ref, inner_ref, back_ref):
    slots, length, width = out_ref.shape
    held, rank, block = down_ref.shape
    fill_masked(pick_ref, ranks_ref, inner_ref, 0, slots, held, rank)
    fill_masked(pick_ref, ranks_ref, back_ref, rank, slots, held, rank)
    down = down_ref[...].reshape(held * rank, block)
    up = up_ref[...].reshape(held * rank, width - block)
    token_part = jnp.dot(back_ref[...], down, preferred_element_type=f32) * adapter_scale
    output_part = jnp.dot(inner_ref[...], up, preferred_element_type=f32) * adapter_scale
    out_ref[:, :, :block] = token_part.astype(bf16).reshape(slots, length, block)
    out_ref[:, :, block:] = output_part.astype(bf16).reshape(slots, length, width - block)


def gradient_body(
    pick_ref, scale_ref, ranks_ref, rows_ref, down_out_ref, up_out_ref, inner_ref, back_ref
):
    slots, length, width = rows_ref.shape
    held, rank, block = down_out_ref.shape
    fill_masked(pick_ref, ranks_ref, inner_ref, 0, slots, held, rank)
    fill_masked(pick_ref, ranks_ref, back_ref, rank, slots, held, rank)
    flat = rows_ref[...].reshape(slots * length, width)
    dims = (((0,), (0,)), ((), ()))
    down = lax.dot_general(back_ref[...], flat[:, :block], dims, preferred_element_type=f32)
    up = lax.dot_general(inner_ref[...], flat[:, block:], dims, preferred_element_type=f32)
    for a in range(held):
        at = slice(a * rank, (a + 1) * rank)
        down_out_ref[a] = down[at] * scale_ref[a]
        up_out_ref[a] = up[at] * scale_ref[a]


def base_body(offsets, place_ref, own_ref, other_ref, weight_ref, out_ref):
    blocks, rows, width = own_ref.shape
    dims = (((1,), (1,)), ((), ()))
    first_core = place_ref[1] == 0
    for b, offset in enumerate(offsets):
        own, other = own_ref[b], other_ref[b]
        low = jnp.where(first_core, own, other)
        high = jnp.where(first_core, other, own)
        pair = jnp.concatenate([low, high], axis=1)
        columns = block_columns(place_ref, offset, blocks, 2 * width)
        part = lax.dot_general(pair, weight_ref[:, columns], dims, preferred_element_type=f32)
        out_ref[...] = part if b == 0 else out_ref[...] + part


def final_body(held, place_ref, index_ref, storage_ref, base_ref, came_ref, *refs):
    part_refs, (token_out_ref, output_ref) = refs[:-2], refs[-2:]
    slots, length, width = came_ref.shape
    block = base_ref.shape[1]
    for j in range(base_ref.shape[0] // length):
        owner = owner_of(place_ref, index_ref, storage_ref, held, j)
        at = slice(j * length, (j + 1) * length)
        came = came_ref[owner].astype(f32)
        token_out_ref[at, :] = (base_ref[at, :] + came[:, :block]).astype(bf16)
        total = came[:, block:]
        for part_ref in part_refs:
            total = total + part_ref[at, :].astype(f32)
        output_ref[at, :] = total.astype(bf16)


def exchange(value, axis, groups=None):
    return lax.all_to_all(
        value, axis, split_axis=0, concat_axis=0, axis_index_groups=groups, tiled=True
    )


def after(value, earlier):
    return lax.optimization_barrier((value, earlier))[0]


def on_device(tokens, weight, down, up, cotangent, sequence_index, storage_row):
    dp_count = lax.axis_size("dp")
    tensor_count = lax.axis_size("tensor")
    chips = tensor_count // 2
    me = lax.axis_index("dp")
    here = lax.axis_index("tensor")
    held, rank, block = down.shape
    out_block = up.shape[2]
    rows = tokens.shape[0]
    seqs = sequence_index.shape[0] // dp_count
    length = rows // seqs
    slots = dp_count
    width = block + out_block
    core = here & 1
    chip = here >> 1
    place = jnp.stack([me * seqs, core, chip, me]).astype(jnp.int32)
    pairs = [[t, t + 1] for t in range(0, tensor_count, 2)]
    same_core = [list(range(c, tensor_count, 2)) for c in range(2)]

    def shape(*dims, dtype=bf16):
        return jax.ShapeDtypeStruct(dims, dtype)

    def moved_along(value, distance):
        perm = [(t, (t + 2 * distance) % tensor_count) for t in range(tensor_count)]
        return lax.ppermute(value, "tensor", perm)

    spread = local_call(
        functools.partial(spread_body, held),
        shape(slots, length, width),
        [SMEM, SMEM, SMEM, VMEM, VMEM],
        moved=3 * slots * length * width,
    )(place, sequence_index, storage_row, tokens, cotangent)
    arrived = exchange(spread, "dp")

    codes = jnp.arange(storage_row.shape[0], dtype=jnp.int32)
    matches = sequence_index[:, None] == codes[None, :]
    seq_rows = jnp.sum(jnp.where(matches, storage_row[None, :], 0), axis=1)
    local = seq_rows - held * me
    local = jnp.where((local >= 0) & (local < held), local, -1)
    pick = jnp.max(local.reshape(dp_count, seqs), axis=1).astype(jnp.int32)
    usage = jnp.sum((pick[:, None] == jnp.arange(held)[None, :]).astype(f32), axis=0)
    scale = adapter_scale / jnp.maximum(usage, 1.0)

    own, send = local_call(
        projection_body,
        (shape(chips, rows, out_block), shape(chips, rows, out_block)),
        [SMEM, VMEM, VMEM],
        flops=2 * rows * block * tensor_count * out_block,
        moved=2 * (rows * block + 2 * block * tensor_count * out_block),
    )(after(place, spread), tokens, weight)
    swap = [(t, t ^ 1) for t in range(tensor_count)]
    came = lax.ppermute(send, "tensor", swap)
    paired = local_call(
        pair_body,
        (shape(rows, out_block),) * chips,
        [VMEM, VMEM],
        moved=6 * chips * rows * out_block,
    )(own, came)
    parts = [paired[0]] + [moved_along(paired[d], d) for d in range(1, chips)]
    arrived, parts = lax.optimization_barrier((arrived, parts))

    half = slots * length // 2
    part = local_call(
        rank_body,
        shape(slots * length, 2 * rank),
        [SMEM, VMEM, VMEM, VMEM],
        flops=2 * slots * length * width * held * rank,
        moved=2 * slots * length * width,
    )(pick, arrived, down, up)
    both = lax.all_gather(part, "tensor", axis_index_groups=pairs)
    mine = lax.dynamic_slice_in_dim(both, core * half, half, axis=1)
    mine = mine.astype(f32).sum(0).astype(bf16).reshape(chips, half // chips, 2 * rank)
    totals = local_call(
        total_body,
        shape(*mine.shape),
        [VMEM],
        moved=4 * half * 2 * rank,
    )(exchange(mine, "tensor", same_core))
    shared = exchange(totals, "tensor", same_core).reshape(half, 2 * rank)
    ranks = lax.all_gather(shared, "tensor", axis_index_groups=pairs).reshape(part.shape)

    masked = pltpu.VMEM((slots * length, held * rank), bf16)
    contributions = local_call(
        expand_body,
        shape(slots, length, width),
        [SMEM, VMEM, VMEM, VMEM],
        [masked, masked],
        flops=2 * slots * length * width * held * rank,
        moved=2 * slots * length * width,
    )(pick, ranks, down, up)
    returned = exchange(contributions, "dp")

    right = left = after(cotangent, contributions)
    pieces, offsets = [right], [0]
    for d in range(1, chips // 2 + 1):
        right = moved_along(right, 1)
        pieces.append(right)
        offsets.append(chips - d)
        if d < chips - d:
            left = moved_along(left, -1)
            pieces.append(left)
            offsets.append(d)
    own_cot = jnp.stack(pieces)
    other_cot = lax.ppermute(own_cot, "tensor", swap)

    grad_down, grad_up = local_call(
        gradient_body,
        (shape(held, rank, block, dtype=f32), shape(held, rank, out_block, dtype=f32)),
        [SMEM, SMEM, VMEM, VMEM],
        [masked, masked],
        flops=2 * slots * length * width * held * rank,
        moved=2 * slots * length * width,
    )(pick, scale, ranks, arrived)
    base = local_call(
        functools.partial(base_body, offsets),
        shape(rows, block, dtype=f32),
        [SMEM, VMEM, VMEM, VMEM],
        flops=2 * rows * block * tensor_count * out_block,
        moved=2 * (2 * rows * tensor_count * out_block),
    )(place, own_cot, other_cot, weight)
    token_gradient, key_value_output = local_call(
        functools.partial(final_body, held),
        (shape(rows, block), shape(rows, out_block)),
        [SMEM, SMEM, SMEM, VMEM, VMEM] + [VMEM] * chips,
        moved=2 * (3 * rows * block + slots * length * width),
    )(place, sequence_index, storage_row, base, returned, *parts)
    return (key_value_output, token_gradient, grad_down, grad_up)


def solution(mesh):
    in_specs = (
        P("dp", "tensor"),
        P("tensor", None),
        P("dp", None, "tensor"),
        P("dp", None, "tensor"),
        P("dp", "tensor"),
        P(),
        P(),
    )
    out_specs = (
        P("dp", "tensor"),
        P("dp", "tensor"),
        P("dp", None, "tensor"),
        P("dp", None, "tensor"),
    )
    return jax.shard_map(
        on_device, mesh=mesh, in_specs=in_specs, out_specs=out_specs, check_vma=False
    )
```

```python
import functools

import jax
import jax.numpy as jnp
from jax import lax
from jax.experimental import pallas as pl
from jax.experimental.pallas import tpu as pltpu
from jax.sharding import PartitionSpec as P

adapter_scale = 0.25
f32 = jnp.float32
bf16 = jnp.bfloat16
SMEM = pl.BlockSpec(memory_space=pltpu.SMEM)
VMEM = pl.BlockSpec(memory_space=pltpu.VMEM)
VMEM_LIMIT = 40 * 1024 * 1024


def local_call(body, out_shape, specs, scratch=(), flops=0, moved=0):
    multiple = isinstance(out_shape, (tuple, list))
    return pl.pallas_call(
        body,
        out_shape=out_shape,
        in_specs=specs,
        out_specs=(VMEM,) * len(out_shape) if multiple else VMEM,
        scratch_shapes=list(scratch),
        compiler_params=pltpu.CompilerParams(vmem_limit_bytes=VMEM_LIMIT),
        cost_estimate=pl.CostEstimate(flops=flops, bytes_accessed=moved, transcendentals=0),
    )


def owner_of(place_ref, index_ref, storage_ref, held, j):
    return storage_ref[index_ref[place_ref[0] + j]] // held


def spread_body(held, place_ref, index_ref, storage_ref, tokens_ref, cot_ref, out_ref):
    slots, length, width = out_ref.shape
    block = tokens_ref.shape[1]
    out_ref[...] = jnp.zeros_like(out_ref)
    for j in range(tokens_ref.shape[0] // length):
        owner = owner_of(place_ref, index_ref, storage_ref, held, j)
        at = slice(j * length, (j + 1) * length)
        out_ref[owner, :, :block] = tokens_ref[at, :]
        out_ref[owner, :, block:] = cot_ref[at, :]


def chip_columns(place_ref, k, blocks, width):
    steps = (0, 2, blocks - 2, blocks // 2)
    chip = place_ref[2] if k < 4 else place_ref[3]
    chip = lax.rem(chip + steps[k % 4], blocks)
    return pl.ds(pl.multiple_of(chip * width, width), width)


def projection_body(place_ref, tokens_ref, weight_ref, own_ref, send_ref):
    blocks, rows, width = own_ref.shape
    core = place_ref[1]
    tokens = tokens_ref[...]
    for b in range(blocks):
        columns = chip_columns(place_ref, b, blocks, 2 * width)
        part = jnp.dot(tokens, weight_ref[:, columns], preferred_element_type=f32).astype(bf16)
        low, high = part[:, :width], part[:, width:]

        @pl.when(core == 0)
        def _():
            own_ref[b] = low
            send_ref[b] = high

        @pl.when(core != 0)
        def _():
            own_ref[b] = high
            send_ref[b] = low


def pair_body(own_ref, came_ref, keep_ref, give_ref):
    half = keep_ref.shape[0]
    for b in range(half):
        keep_ref[b] = (own_ref[b].astype(f32) + came_ref[b].astype(f32)).astype(bf16)
        other = own_ref[half + b].astype(f32) + came_ref[half + b].astype(f32)
        give_ref[b] = other.astype(bf16)


def neighbour_body(keep_ref, came_ref, *out_refs):
    for b, out_ref in enumerate(out_refs):
        out_ref[...] = (keep_ref[b].astype(f32) + came_ref[b].astype(f32)).astype(bf16)


def pack_body(*refs):
    for b, ref in enumerate(refs[:-1]):
        refs[-1][b] = ref[...]


def rank_body(pick_ref, rows_ref, down_ref, up_ref, out_ref):
    slots, length, width = rows_ref.shape
    held, rank, block = down_ref.shape
    flat = rows_ref[...].reshape(slots * length, width)
    dims = (((1,), (1,)), ((), ()))
    inner = [
        lax.dot_general(flat[:, :block], down_ref[a], dims, preferred_element_type=f32)
        for a in range(held)
    ]
    back = [
        lax.dot_general(flat[:, block:], up_ref[a], dims, preferred_element_type=f32)
        for a in range(held)
    ]
    joined = [jnp.concatenate([inner[a], back[a]], axis=1) for a in range(held)]
    for s in range(slots):
        at = slice(s * length, (s + 1) * length)
        value = jnp.zeros((length, 2 * rank), f32)
        for a in range(held):
            value = jnp.where(pick_ref[s] == a, joined[a][at], value)
        out_ref[at, :] = value.astype(bf16)


def total_body(parts_ref, out_ref):
    total = jnp.sum(parts_ref[...].astype(f32), axis=0).astype(bf16)
    for b in range(out_ref.shape[0]):
        out_ref[b] = total


def fill_masked(pick_ref, ranks_ref, masked_ref, left, slots, held, rank):
    length = ranks_ref.shape[0] // slots
    for s in range(slots):
        at = slice(s * length, (s + 1) * length)
        block = ranks_ref[at, :][:, left : left + rank]
        for a in range(held):
            masked_ref[at, a * rank : (a + 1) * rank] = jnp.where(
                pick_ref[s] == a, block, jnp.zeros_like(block)
            )


def expand_body(pick_ref, ranks_ref, down_ref, up_ref, out_ref, inner_ref, back_ref):
    slots, length, width = out_ref.shape
    held, rank, block = down_ref.shape
    fill_masked(pick_ref, ranks_ref, inner_ref, 0, slots, held, rank)
    fill_masked(pick_ref, ranks_ref, back_ref, rank, slots, held, rank)
    down = down_ref[...].reshape(held * rank, block)
    up = up_ref[...].reshape(held * rank, width - block)
    token_part = jnp.dot(back_ref[...], down, preferred_element_type=f32) * adapter_scale
    output_part = jnp.dot(inner_ref[...], up, preferred_element_type=f32) * adapter_scale
    out_ref[:, :, :block] = token_part.astype(bf16).reshape(slots, length, block)
    out_ref[:, :, block:] = output_part.astype(bf16).reshape(slots, length, width - block)


def gradient_body(
    pick_ref, scale_ref, ranks_ref, rows_ref, down_out_ref, up_out_ref, inner_ref, back_ref
):
    slots, length, width = rows_ref.shape
    held, rank, block = down_out_ref.shape
    fill_masked(pick_ref, ranks_ref, inner_ref, 0, slots, held, rank)
    fill_masked(pick_ref, ranks_ref, back_ref, rank, slots, held, rank)
    flat = rows_ref[...].reshape(slots * length, width)
    dims = (((0,), (0,)), ((), ()))
    down = lax.dot_general(back_ref[...], flat[:, :block], dims, preferred_element_type=f32)
    up = lax.dot_general(inner_ref[...], flat[:, block:], dims, preferred_element_type=f32)
    for a in range(held):
        at = slice(a * rank, (a + 1) * rank)
        down_out_ref[a] = down[at] * scale_ref[a]
        up_out_ref[a] = up[at] * scale_ref[a]


def base_body(place_ref, near_ref, near_other_ref, far_ref, far_other_ref, weight_ref, out_ref):
    blocks, rows, width = near_ref.shape
    dims = (((1,), (1,)), ((), ()))
    first_core = place_ref[1] == 0
    for k in range(2 * blocks):
        own_ref, other_ref = (near_ref, near_other_ref) if k < blocks else (far_ref, far_other_ref)
        own, other = own_ref[k % blocks], other_ref[k % blocks]
        low = jnp.where(first_core, own, other)
        high = jnp.where(first_core, other, own)
        pair = jnp.concatenate([low, high], axis=1)
        columns = chip_columns(place_ref, k, 2 * blocks, 2 * width)
        part = lax.dot_general(pair, weight_ref[:, columns], dims, preferred_element_type=f32)
        out_ref[...] = part if k == 0 else out_ref[...] + part


def final_body(held, place_ref, index_ref, storage_ref, base_ref, came_ref, *refs):
    part_refs, (token_out_ref, output_ref) = refs[:-2], refs[-2:]
    slots, length, width = came_ref.shape
    block = base_ref.shape[1]
    for j in range(base_ref.shape[0] // length):
        owner = owner_of(place_ref, index_ref, storage_ref, held, j)
        at = slice(j * length, (j + 1) * length)
        came = came_ref[owner].astype(f32)
        token_out_ref[at, :] = (base_ref[at, :] + came[:, :block]).astype(bf16)
        total = came[:, block:]
        for part_ref in part_refs:
            total = total + part_ref[at, :].astype(f32)
        output_ref[at, :] = total.astype(bf16)


def exchange(value, axis, groups=None):
    return lax.all_to_all(
        value, axis, split_axis=0, concat_axis=0, axis_index_groups=groups, tiled=True
    )


def after(value, earlier):
    return lax.optimization_barrier((value, earlier))[0]


def on_device(tokens, weight, down, up, cotangent, sequence_index, storage_row):
    dp_count = lax.axis_size("dp")
    tensor_count = lax.axis_size("tensor")
    chips = tensor_count // 2
    me = lax.axis_index("dp")
    here = lax.axis_index("tensor")
    held, rank, block = down.shape
    out_block = up.shape[2]
    rows = tokens.shape[0]
    seqs = sequence_index.shape[0] // dp_count
    length = rows // seqs
    slots = dp_count
    width = block + out_block
    core = here & 1
    chip = here >> 1
    place = jnp.stack([me * seqs, core, chip, chip ^ 1]).astype(jnp.int32)
    pairs = [[t, t + 1] for t in range(0, tensor_count, 2)]
    same_core = [list(range(c, tensor_count, 2)) for c in range(2)]

    def shape(*dims, dtype=bf16):
        return jax.ShapeDtypeStruct(dims, dtype)

    def moved_along(value, distance):
        perm = [(t, (t + 2 * distance) % tensor_count) for t in range(tensor_count)]
        return lax.ppermute(value, "tensor", perm)

    spread = local_call(
        functools.partial(spread_body, held),
        shape(slots, length, width),
        [SMEM, SMEM, SMEM, VMEM, VMEM],
        moved=3 * slots * length * width,
    )(place, sequence_index, storage_row, tokens, cotangent)
    arrived = exchange(spread, "dp")

    codes = jnp.arange(storage_row.shape[0], dtype=jnp.int32)
    matches = sequence_index[:, None] == codes[None, :]
    seq_rows = jnp.sum(jnp.where(matches, storage_row[None, :], 0), axis=1)
    local = seq_rows - held * me
    local = jnp.where((local >= 0) & (local < held), local, -1)
    pick = jnp.max(local.reshape(dp_count, seqs), axis=1).astype(jnp.int32)
    usage = jnp.sum((pick[:, None] == jnp.arange(held)[None, :]).astype(f32), axis=0)
    scale = adapter_scale / jnp.maximum(usage, 1.0)

    swap = [(t, t ^ 1) for t in range(tensor_count)]
    across = [(t, t ^ 2) for t in range(tensor_count)]
    quarter = chips // 2
    cot = after(cotangent, spread)
    near = local_call(
        pack_body,
        shape(quarter, rows, out_block),
        [VMEM] * quarter,
        moved=4 * quarter * rows * out_block,
    )(cot, moved_along(cot, -2), moved_along(cot, 2), moved_along(cot, quarter))
    far = lax.ppermute(near, "tensor", across)
    near_other = lax.ppermute(near, "tensor", swap)
    far_other = lax.ppermute(far, "tensor", swap)

    own, send = local_call(
        projection_body,
        (shape(chips, rows, out_block), shape(chips, rows, out_block)),
        [SMEM, VMEM, VMEM],
        flops=2 * rows * block * tensor_count * out_block,
        moved=2 * (rows * block + 2 * block * tensor_count * out_block),
    )(after(place, spread), tokens, weight)
    came = lax.ppermute(send, "tensor", swap)
    keep, give = local_call(
        pair_body,
        (shape(quarter, rows, out_block),) * 2,
        [VMEM, VMEM],
        moved=6 * chips * rows * out_block,
    )(own, came)
    base = local_call(
        base_body,
        shape(rows, block, dtype=f32),
        [SMEM, VMEM, VMEM, VMEM, VMEM, VMEM],
        flops=2 * rows * block * tensor_count * out_block,
        moved=2 * (2 * rows * tensor_count * out_block),
    )(place, near, near_other, far, far_other, weight)
    arrived, base, keep, give = lax.optimization_barrier((arrived, base, keep, give))

    half = slots * length // 2
    part = local_call(
        rank_body,
        shape(slots * length, 2 * rank),
        [SMEM, VMEM, VMEM, VMEM],
        flops=2 * slots * length * width * held * rank,
        moved=2 * slots * length * width,
    )(pick, arrived, down, up)
    both = lax.all_gather(part, "tensor", axis_index_groups=pairs)
    mine = lax.dynamic_slice_in_dim(both, core * half, half, axis=1)
    mine = mine.astype(f32).sum(0).astype(bf16).reshape(chips, half // chips, 2 * rank)
    totals = local_call(
        total_body,
        shape(*mine.shape),
        [VMEM],
        moved=4 * half * 2 * rank,
    )(exchange(mine, "tensor", same_core))
    shared = exchange(totals, "tensor", same_core).reshape(half, 2 * rank)
    ranks = lax.all_gather(shared, "tensor", axis_index_groups=pairs).reshape(part.shape)

    masked = pltpu.VMEM((slots * length, held * rank), bf16)
    contributions = local_call(
        expand_body,
        shape(slots, length, width),
        [SMEM, VMEM, VMEM, VMEM],
        [masked, masked],
        flops=2 * slots * length * width * held * rank,
        moved=2 * slots * length * width,
    )(pick, ranks, down, up)
    returned = exchange(contributions, "dp")

    crossed = lax.ppermute(after(give, contributions), "tensor", across)
    summed = local_call(
        neighbour_body,
        (shape(rows, out_block),) * quarter,
        [VMEM, VMEM],
        moved=6 * quarter * rows * out_block,
    )(keep, crossed)
    parts = [summed[0]]
    for value, distance in zip(summed[1:], (2, -2, quarter)):
        parts.append(moved_along(value, distance))

    grad_down, grad_up = local_call(
        gradient_body,
        (shape(held, rank, block, dtype=f32), shape(held, rank, out_block, dtype=f32)),
        [SMEM, SMEM, VMEM, VMEM],
        [masked, masked],
        flops=2 * slots * length * width * held * rank,
        moved=2 * slots * length * width,
    )(pick, scale, ranks, arrived)
    token_gradient, key_value_output = local_call(
        functools.partial(final_body, held),
        (shape(rows, block), shape(rows, out_block)),
        [SMEM, SMEM, SMEM, VMEM, VMEM] + [VMEM] * quarter,
        moved=2 * (3 * rows * block + slots * length * width),
    )(place, sequence_index, storage_row, base, returned, *parts)
    return (key_value_output, token_gradient, grad_down, grad_up)


def solution(mesh):
    in_specs = (
        P("dp", "tensor"),
        P("tensor", None),
        P("dp", None, "tensor"),
        P("dp", None, "tensor"),
        P("dp", "tensor"),
        P(),
        P(),
    )
    out_specs = (
        P("dp", "tensor"),
        P("dp", "tensor"),
        P("dp", None, "tensor"),
        P("dp", None, "tensor"),
    )
    return jax.shard_map(
        on_device, mesh=mesh, in_specs=in_specs, out_specs=out_specs, check_vma=False
    )
```

```python
import functools

import jax
import jax.numpy as jnp
from jax import lax
from jax.experimental import pallas as pl
from jax.experimental.pallas import tpu as pltpu
from jax.sharding import PartitionSpec as P

adapter_scale = 0.25
f32 = jnp.float32
bf16 = jnp.bfloat16
SMEM = pl.BlockSpec(memory_space=pltpu.SMEM)
VMEM = pl.BlockSpec(memory_space=pltpu.VMEM)
VMEM_LIMIT = 16 * 1024 * 1024
HBM_LIMIT = 60 * 1024 * 1024
ANY = pl.BlockSpec(memory_space=pl.ANY)


def local_call(body, out_shape, specs, scratch=(), flops=0, moved=0, out=VMEM, limit=VMEM_LIMIT):
    multiple = isinstance(out_shape, (tuple, list))
    return pl.pallas_call(
        body,
        out_shape=out_shape,
        in_specs=specs,
        out_specs=(out,) * len(out_shape) if multiple else out,
        scratch_shapes=list(scratch),
        compiler_params=pltpu.CompilerParams(vmem_limit_bytes=limit),
        cost_estimate=pl.CostEstimate(flops=flops, bytes_accessed=moved, transcendentals=0),
    )


def owner_of(place_ref, index_ref, storage_ref, held, j):
    return storage_ref[index_ref[place_ref[0] + j]] // held


def spread_body(
    held,
    place_ref,
    index_hbm,
    storage_hbm,
    tokens_hbm,
    cot_hbm,
    out_hbm,
    index_ref,
    storage_ref,
    source_ref,
    table_sems,
    token_sems,
    cot_sems,
):
    slots, length, width = out_hbm.shape
    block = tokens_hbm.shape[1]
    tables = [
        pltpu.make_async_copy(index_hbm, index_ref, table_sems.at[0]),
        pltpu.make_async_copy(storage_hbm, storage_ref, table_sems.at[1]),
    ]
    for table in tables:
        table.start()
    seqs = tokens_hbm.shape[0] // length
    for s in range(slots):
        source_ref[s] = s % seqs
    for table in tables:
        table.wait()
    for j in range(seqs):
        source_ref[owner_of(place_ref, index_ref, storage_ref, held, j)] = j
    copies = []
    for s in range(slots):
        at = pl.ds(pl.multiple_of(source_ref[s] * length, length), length)
        copies.append(
            pltpu.make_async_copy(
                tokens_hbm.at[at, :], out_hbm.at[s, :, pl.ds(0, block)], token_sems.at[s]
            )
        )
        copies.append(
            pltpu.make_async_copy(
                cot_hbm.at[at, :], out_hbm.at[s, :, pl.ds(block, width - block)], cot_sems.at[s]
            )
        )
        copies[-2].start()
        copies[-1].start()
    for copy in copies:
        copy.wait()


def chip_columns(place_ref, k, blocks, width):
    steps = (0, 2, blocks - 2, blocks // 2)
    chip = place_ref[2] if k < 4 else place_ref[3]
    chip = lax.rem(chip + steps[k % 4], blocks)
    return pl.ds(pl.multiple_of(chip * width, width), width)


def projection_body(place_ref, tokens_ref, weight_ref, own_ref, send_ref):
    blocks, rows, width = own_ref.shape
    core = place_ref[1]
    tokens = tokens_ref[...]
    for b in range(blocks):
        columns = chip_columns(place_ref, b, blocks, 2 * width)
        part = jnp.dot(tokens, weight_ref[:, columns], preferred_element_type=f32).astype(bf16)
        low, high = part[:, :width], part[:, width:]

        @pl.when(core == 0)
        def _():
            own_ref[b] = low
            send_ref[b] = high

        @pl.when(core != 0)
        def _():
            own_ref[b] = high
            send_ref[b] = low


def pair_body(own_ref, came_ref, keep_ref, give_ref):
    half = keep_ref.shape[0]
    for b in range(half):
        keep_ref[b] = (own_ref[b].astype(f32) + came_ref[b].astype(f32)).astype(bf16)
        other = own_ref[half + b].astype(f32) + came_ref[half + b].astype(f32)
        give_ref[b] = other.astype(bf16)


def neighbour_body(keep_ref, came_ref, *out_refs):
    for b, out_ref in enumerate(out_refs):
        out_ref[...] = (keep_ref[b].astype(f32) + came_ref[b].astype(f32)).astype(bf16)


def pack_body(*refs):
    for b, ref in enumerate(refs[:-1]):
        refs[-1][b] = ref[...]


def rank_body(pick_ref, rows_ref, down_ref, up_ref, out_ref):
    slots, length, width = rows_ref.shape
    held, rank, block = down_ref.shape
    flat = rows_ref[...].reshape(slots * length, width)
    dims = (((1,), (1,)), ((), ()))
    inner = [
        lax.dot_general(flat[:, :block], down_ref[a], dims, preferred_element_type=f32)
        for a in range(held)
    ]
    back = [
        lax.dot_general(flat[:, block:], up_ref[a], dims, preferred_element_type=f32)
        for a in range(held)
    ]
    joined = [jnp.concatenate([inner[a], back[a]], axis=1) for a in range(held)]
    for s in range(slots):
        at = slice(s * length, (s + 1) * length)
        value = jnp.zeros((length, 2 * rank), f32)
        for a in range(held):
            value = jnp.where(pick_ref[s] == a, joined[a][at], value)
        out_ref[at, :] = value.astype(bf16)


def total_body(parts_ref, out_ref):
    total = jnp.sum(parts_ref[...].astype(f32), axis=0).astype(bf16)
    for b in range(out_ref.shape[0]):
        out_ref[b] = total


def fill_masked(pick_ref, ranks_ref, masked_ref, left, slots, held, rank):
    length = ranks_ref.shape[0] // slots
    for s in range(slots):
        at = slice(s * length, (s + 1) * length)
        block = ranks_ref[at, :][:, left : left + rank]
        for a in range(held):
            masked_ref[at, a * rank : (a + 1) * rank] = jnp.where(
                pick_ref[s] == a, block, jnp.zeros_like(block)
            )


def expand_body(pick_ref, ranks_ref, down_ref, up_ref, out_ref, inner_ref, back_ref):
    slots, length, width = out_ref.shape
    held, rank, block = down_ref.shape
    fill_masked(pick_ref, ranks_ref, inner_ref, 0, slots, held, rank)
    fill_masked(pick_ref, ranks_ref, back_ref, rank, slots, held, rank)
    down = down_ref[...].reshape(held * rank, block)
    up = up_ref[...].reshape(held * rank, width - block)
    token_part = jnp.dot(back_ref[...], down, preferred_element_type=f32) * adapter_scale
    output_part = jnp.dot(inner_ref[...], up, preferred_element_type=f32) * adapter_scale
    out_ref[:, :, :block] = token_part.astype(bf16).reshape(slots, length, block)
    out_ref[:, :, block:] = output_part.astype(bf16).reshape(slots, length, width - block)


def gradient_body(
    pick_ref, scale_ref, ranks_ref, rows_ref, down_out_ref, up_out_ref, inner_ref, back_ref
):
    slots, length, width = rows_ref.shape
    held, rank, block = down_out_ref.shape
    fill_masked(pick_ref, ranks_ref, inner_ref, 0, slots, held, rank)
    fill_masked(pick_ref, ranks_ref, back_ref, rank, slots, held, rank)
    flat = rows_ref[...].reshape(slots * length, width)
    dims = (((0,), (0,)), ((), ()))
    down = lax.dot_general(back_ref[...], flat[:, :block], dims, preferred_element_type=f32)
    up = lax.dot_general(inner_ref[...], flat[:, block:], dims, preferred_element_type=f32)
    for a in range(held):
        at = slice(a * rank, (a + 1) * rank)
        down_out_ref[a] = down[at] * scale_ref[a]
        up_out_ref[a] = up[at] * scale_ref[a]


def base_body(place_ref, near_ref, near_other_ref, far_ref, far_other_ref, weight_ref, out_ref):
    blocks, rows, width = near_ref.shape
    dims = (((1,), (1,)), ((), ()))
    first_core = place_ref[1] == 0
    for k in range(2 * blocks):
        own_ref, other_ref = (near_ref, near_other_ref) if k < blocks else (far_ref, far_other_ref)
        own, other = own_ref[k % blocks], other_ref[k % blocks]
        low = jnp.where(first_core, own, other)
        high = jnp.where(first_core, other, own)
        pair = jnp.concatenate([low, high], axis=1)
        columns = chip_columns(place_ref, k, 2 * blocks, 2 * width)
        part = lax.dot_general(pair, weight_ref[:, columns], dims, preferred_element_type=f32)
        out_ref[...] = part if k == 0 else out_ref[...] + part


def final_body(held, place_ref, index_ref, storage_ref, base_ref, came_ref, *refs):
    part_refs, (token_out_ref, output_ref) = refs[:-2], refs[-2:]
    slots, length, width = came_ref.shape
    block = base_ref.shape[1]
    for j in range(base_ref.shape[0] // length):
        owner = owner_of(place_ref, index_ref, storage_ref, held, j)
        at = slice(j * length, (j + 1) * length)
        came = came_ref[owner].astype(f32)
        token_out_ref[at, :] = (base_ref[at, :] + came[:, :block]).astype(bf16)
        total = came[:, block:]
        for part_ref in part_refs:
            total = total + part_ref[at, :].astype(f32)
        output_ref[at, :] = total.astype(bf16)


def exchange(value, axis, groups=None):
    return lax.all_to_all(
        value, axis, split_axis=0, concat_axis=0, axis_index_groups=groups, tiled=True
    )


def after(value, earlier):
    return lax.optimization_barrier((value, earlier))[0]


def on_device(tokens, weight, down, up, cotangent, sequence_index, storage_row):
    dp_count = lax.axis_size("dp")
    tensor_count = lax.axis_size("tensor")
    chips = tensor_count // 2
    me = lax.axis_index("dp")
    here = lax.axis_index("tensor")
    held, rank, block = down.shape
    out_block = up.shape[2]
    rows = tokens.shape[0]
    seqs = sequence_index.shape[0] // dp_count
    length = rows // seqs
    slots = dp_count
    width = block + out_block
    core = here & 1
    chip = here >> 1
    place = jnp.stack([me * seqs, core, chip, chip ^ 1]).astype(jnp.int32)
    pairs = [[t, t + 1] for t in range(0, tensor_count, 2)]
    same_core = [list(range(c, tensor_count, 2)) for c in range(2)]

    def shape(*dims, dtype=bf16):
        return jax.ShapeDtypeStruct(dims, dtype)

    def moved_along(value, distance):
        perm = [(t, (t + 2 * distance) % tensor_count) for t in range(tensor_count)]
        return lax.ppermute(value, "tensor", perm)

    spread = local_call(
        functools.partial(spread_body, held),
        shape(slots, length, width),
        [SMEM, ANY, ANY, ANY, ANY],
        [
            pltpu.SMEM(sequence_index.shape, jnp.int32),
            pltpu.SMEM(storage_row.shape, jnp.int32),
            pltpu.SMEM((slots,), jnp.int32),
            pltpu.SemaphoreType.DMA((2,)),
            pltpu.SemaphoreType.DMA((slots,)),
            pltpu.SemaphoreType.DMA((slots,)),
        ],
        moved=3 * slots * length * width,
        out=ANY,
        limit=HBM_LIMIT,
    )(place, sequence_index, storage_row, tokens, cotangent)
    arrived = exchange(spread, "dp")

    codes = jnp.arange(storage_row.shape[0], dtype=jnp.int32)
    matches = sequence_index[:, None] == codes[None, :]
    seq_rows = jnp.sum(jnp.where(matches, storage_row[None, :], 0), axis=1)
    local = seq_rows - held * me
    local = jnp.where((local >= 0) & (local < held), local, -1)
    pick = jnp.max(local.reshape(dp_count, seqs), axis=1).astype(jnp.int32)
    usage = jnp.sum((pick[:, None] == jnp.arange(held)[None, :]).astype(f32), axis=0)
    scale = adapter_scale / jnp.maximum(usage, 1.0)

    swap = [(t, t ^ 1) for t in range(tensor_count)]
    across = [(t, t ^ 2) for t in range(tensor_count)]
    quarter = chips // 2
    cot = after(cotangent, spread)
    near = local_call(
        pack_body,
        shape(quarter, rows, out_block),
        [VMEM] * quarter,
        moved=4 * quarter * rows * out_block,
    )(cot, moved_along(cot, -2), moved_along(cot, 2), moved_along(cot, quarter))
    far = lax.ppermute(near, "tensor", across)
    near_other = lax.ppermute(near, "tensor", swap)
    far_other = lax.ppermute(far, "tensor", swap)

    own, send = local_call(
        projection_body,
        (shape(chips, rows, out_block), shape(chips, rows, out_block)),
        [SMEM, VMEM, VMEM],
        flops=2 * rows * block * tensor_count * out_block,
        moved=2 * (rows * block + 2 * block * tensor_count * out_block),
    )(after(place, near), tokens, weight)
    came = lax.ppermute(send, "tensor", swap)
    arrived, near_other, far_other, own, came = lax.optimization_barrier(
        (arrived, near_other, far_other, own, came)
    )

    half = slots * length // 2
    part = local_call(
        rank_body,
        shape(slots * length, 2 * rank),
        [SMEM, VMEM, VMEM, VMEM],
        flops=2 * slots * length * width * held * rank,
        moved=2 * slots * length * width,
    )(pick, arrived, down, up)
    both = lax.all_gather(part, "tensor", axis_index_groups=pairs)
    mine = lax.dynamic_slice_in_dim(both, core * half, half, axis=1)
    mine = mine.astype(f32).sum(0).astype(bf16).reshape(chips, half // chips, 2 * rank)
    base = local_call(
        base_body,
        shape(rows, block, dtype=f32),
        [SMEM, VMEM, VMEM, VMEM, VMEM, VMEM],
        flops=2 * rows * block * tensor_count * out_block,
        moved=2 * (2 * rows * tensor_count * out_block),
    )(after(place, mine), near, near_other, far, far_other, weight)
    pieces, base = lax.optimization_barrier((exchange(mine, "tensor", same_core), base))
    totals = local_call(
        total_body,
        shape(*mine.shape),
        [VMEM],
        moved=4 * half * 2 * rank,
    )(pieces)
    own, totals = lax.optimization_barrier((own, totals))
    keep, give = local_call(
        pair_body,
        (shape(quarter, rows, out_block),) * 2,
        [VMEM, VMEM],
        moved=6 * chips * rows * out_block,
    )(own, came)
    shared, keep, give = lax.optimization_barrier(
        (exchange(totals, "tensor", same_core), keep, give)
    )
    shared = shared.reshape(half, 2 * rank)
    ranks = lax.all_gather(shared, "tensor", axis_index_groups=pairs).reshape(part.shape)

    masked = pltpu.VMEM((slots * length, held * rank), bf16)
    contributions = local_call(
        expand_body,
        shape(slots, length, width),
        [SMEM, VMEM, VMEM, VMEM],
        [masked, masked],
        flops=2 * slots * length * width * held * rank,
        moved=2 * slots * length * width,
        limit=HBM_LIMIT,
    )(pick, ranks, down, up)
    returned = exchange(contributions, "dp")

    crossed = lax.ppermute(after(give, contributions), "tensor", across)
    summed = local_call(
        neighbour_body,
        (shape(rows, out_block),) * quarter,
        [VMEM, VMEM],
        moved=6 * quarter * rows * out_block,
    )(keep, crossed)
    parts = [summed[0]]
    for value, distance in zip(summed[1:], (2, -2, quarter)):
        parts.append(moved_along(value, distance))

    grad_down, grad_up = local_call(
        gradient_body,
        (shape(held, rank, block, dtype=f32), shape(held, rank, out_block, dtype=f32)),
        [SMEM, SMEM, VMEM, VMEM],
        [masked, masked],
        flops=2 * slots * length * width * held * rank,
        moved=2 * slots * length * width,
    )(pick, scale, ranks, arrived)
    token_gradient, key_value_output = local_call(
        functools.partial(final_body, held),
        (shape(rows, block), shape(rows, out_block)),
        [SMEM, SMEM, SMEM, VMEM, VMEM] + [VMEM] * quarter,
        moved=2 * (3 * rows * block + slots * length * width),
        limit=HBM_LIMIT,
    )(place, sequence_index, storage_row, base, returned, *parts)
    return (key_value_output, token_gradient, grad_down, grad_up)


def solution(mesh):
    in_specs = (
        P("dp", "tensor"),
        P("tensor", None),
        P("dp", None, "tensor"),
        P("dp", None, "tensor"),
        P("dp", "tensor"),
        P(),
        P(),
    )
    out_specs = (
        P("dp", "tensor"),
        P("dp", "tensor"),
        P("dp", None, "tensor"),
        P("dp", None, "tensor"),
    )
    return jax.shard_map(
        on_device, mesh=mesh, in_specs=in_specs, out_specs=out_specs, check_vma=False
    )
```

```python
import functools

import jax
import jax.numpy as jnp
from jax import lax
from jax.experimental import pallas as pl
from jax.experimental.pallas import tpu as pltpu
from jax.sharding import PartitionSpec as P

adapter_scale = 0.25
f32 = jnp.float32
bf16 = jnp.bfloat16
SMEM = pl.BlockSpec(memory_space=pltpu.SMEM)
VMEM = pl.BlockSpec(memory_space=pltpu.VMEM)
VMEM_LIMIT = 16 * 1024 * 1024
HBM_LIMIT = 60 * 1024 * 1024


def local_call(body, out_shape, specs, scratch=(), flops=0, moved=0, limit=VMEM_LIMIT):
    multiple = isinstance(out_shape, (tuple, list))
    return pl.pallas_call(
        body,
        out_shape=out_shape,
        in_specs=specs,
        out_specs=(VMEM,) * len(out_shape) if multiple else VMEM,
        scratch_shapes=list(scratch),
        compiler_params=pltpu.CompilerParams(vmem_limit_bytes=limit),
        cost_estimate=pl.CostEstimate(flops=flops, bytes_accessed=moved, transcendentals=0),
    )


def owner_of(place_ref, index_ref, storage_ref, held, j):
    return storage_ref[index_ref[place_ref[0] + j]] // held


def spread_body(held, place_ref, index_ref, storage_ref, tokens_ref, cot_ref, out_ref):
    slots, length, width = out_ref.shape
    block = tokens_ref.shape[1]
    out_ref[...] = jnp.zeros_like(out_ref)
    for j in range(tokens_ref.shape[0] // length):
        owner = owner_of(place_ref, index_ref, storage_ref, held, j)
        at = slice(j * length, (j + 1) * length)
        out_ref[owner, :, :block] = tokens_ref[at, :]
        out_ref[owner, :, block:] = cot_ref[at, :]


def chip_columns(place_ref, k, blocks, width):
    steps = (0, 2, blocks - 2, blocks // 2)
    chip = place_ref[2] if k < 4 else place_ref[3]
    chip = lax.rem(chip + steps[k % 4], blocks)
    return pl.ds(pl.multiple_of(chip * width, width), width)


def projection_body(place_ref, tokens_ref, weight_ref, own_ref, send_ref):
    blocks, rows, width = own_ref.shape
    core = place_ref[1]
    tokens = tokens_ref[...]
    for b in range(blocks):
        columns = chip_columns(place_ref, b, blocks, 2 * width)
        part = jnp.dot(tokens, weight_ref[:, columns], preferred_element_type=f32).astype(bf16)
        low, high = part[:, :width], part[:, width:]

        @pl.when(core == 0)
        def _():
            own_ref[b] = low
            send_ref[b] = high

        @pl.when(core != 0)
        def _():
            own_ref[b] = high
            send_ref[b] = low


def pair_body(own_ref, came_ref, keep_ref, give_ref):
    half = keep_ref.shape[0]
    for b in range(half):
        keep_ref[b] = (own_ref[b].astype(f32) + came_ref[b].astype(f32)).astype(bf16)
        other = own_ref[half + b].astype(f32) + came_ref[half + b].astype(f32)
        give_ref[b] = other.astype(bf16)


def neighbour_body(keep_ref, came_ref, *out_refs):
    for b, out_ref in enumerate(out_refs):
        out_ref[...] = (keep_ref[b].astype(f32) + came_ref[b].astype(f32)).astype(bf16)


def pack_body(*refs):
    for b, ref in enumerate(refs[:-1]):
        refs[-1][b] = ref[...]


def rank_body(pick_ref, rows_ref, down_ref, up_ref, out_ref):
    slots, length, width = rows_ref.shape
    held, rank, block = down_ref.shape
    flat = rows_ref[...].reshape(slots * length, width)
    dims = (((1,), (1,)), ((), ()))
    inner = [
        lax.dot_general(flat[:, :block], down_ref[a], dims, preferred_element_type=f32)
        for a in range(held)
    ]
    back = [
        lax.dot_general(flat[:, block:], up_ref[a], dims, preferred_element_type=f32)
        for a in range(held)
    ]
    joined = [jnp.concatenate([inner[a], back[a]], axis=1) for a in range(held)]
    for s in range(slots):
        at = slice(s * length, (s + 1) * length)
        value = jnp.zeros((length, 2 * rank), f32)
        for a in range(held):
            value = jnp.where(pick_ref[s] == a, joined[a][at], value)
        out_ref[at, :] = value.astype(bf16)


def total_body(parts_ref, out_ref):
    total = jnp.sum(parts_ref[...].astype(f32), axis=0).astype(bf16)
    for b in range(out_ref.shape[0]):
        out_ref[b] = total


def fill_masked(pick_ref, ranks_ref, masked_ref, left, slots, held, rank):
    length = ranks_ref.shape[0] // slots
    for s in range(slots):
        at = slice(s * length, (s + 1) * length)
        block = ranks_ref[at, :][:, left : left + rank]
        for a in range(held):
            masked_ref[at, a * rank : (a + 1) * rank] = jnp.where(
                pick_ref[s] == a, block, jnp.zeros_like(block)
            )


def expand_body(pick_ref, ranks_ref, down_ref, up_ref, out_ref, inner_ref, back_ref):
    slots, length, width = out_ref.shape
    held, rank, block = down_ref.shape
    fill_masked(pick_ref, ranks_ref, inner_ref, 0, slots, held, rank)
    fill_masked(pick_ref, ranks_ref, back_ref, rank, slots, held, rank)
    down = down_ref[...].reshape(held * rank, block)
    up = up_ref[...].reshape(held * rank, width - block)
    token_part = jnp.dot(back_ref[...], down, preferred_element_type=f32) * adapter_scale
    output_part = jnp.dot(inner_ref[...], up, preferred_element_type=f32) * adapter_scale
    out_ref[:, :, :block] = token_part.astype(bf16).reshape(slots, length, block)
    out_ref[:, :, block:] = output_part.astype(bf16).reshape(slots, length, width - block)


def gradient_body(
    pick_ref, scale_ref, ranks_ref, rows_ref, down_out_ref, up_out_ref, inner_ref, back_ref
):
    slots, length, width = rows_ref.shape
    held, rank, block = down_out_ref.shape
    fill_masked(pick_ref, ranks_ref, inner_ref, 0, slots, held, rank)
    fill_masked(pick_ref, ranks_ref, back_ref, rank, slots, held, rank)
    flat = rows_ref[...].reshape(slots * length, width)
    dims = (((0,), (0,)), ((), ()))
    down = lax.dot_general(back_ref[...], flat[:, :block], dims, preferred_element_type=f32)
    up = lax.dot_general(inner_ref[...], flat[:, block:], dims, preferred_element_type=f32)
    for a in range(held):
        at = slice(a * rank, (a + 1) * rank)
        down_out_ref[a] = down[at] * scale_ref[a]
        up_out_ref[a] = up[at] * scale_ref[a]


def base_body(place_ref, near_ref, near_other_ref, far_ref, far_other_ref, weight_ref, out_ref):
    blocks, rows, width = near_ref.shape
    dims = (((1,), (1,)), ((), ()))
    first_core = place_ref[1] == 0
    for k in range(2 * blocks):
        own_ref, other_ref = (near_ref, near_other_ref) if k < blocks else (far_ref, far_other_ref)
        own, other = own_ref[k % blocks], other_ref[k % blocks]
        low = jnp.where(first_core, own, other)
        high = jnp.where(first_core, other, own)
        pair = jnp.concatenate([low, high], axis=1)
        columns = chip_columns(place_ref, k, 2 * blocks, 2 * width)
        part = lax.dot_general(pair, weight_ref[:, columns], dims, preferred_element_type=f32)
        out_ref[...] = part if k == 0 else out_ref[...] + part


def final_body(held, place_ref, index_ref, storage_ref, base_ref, came_ref, *refs):
    part_refs, (token_out_ref, output_ref) = refs[:-2], refs[-2:]
    slots, length, width = came_ref.shape
    block = base_ref.shape[1]
    for j in range(base_ref.shape[0] // length):
        owner = owner_of(place_ref, index_ref, storage_ref, held, j)
        at = slice(j * length, (j + 1) * length)
        came = came_ref[owner].astype(f32)
        token_out_ref[at, :] = (base_ref[at, :] + came[:, :block]).astype(bf16)
        total = came[:, block:]
        for part_ref in part_refs:
            total = total + part_ref[at, :].astype(f32)
        output_ref[at, :] = total.astype(bf16)


def exchange(value, axis, groups=None):
    return lax.all_to_all(
        value, axis, split_axis=0, concat_axis=0, axis_index_groups=groups, tiled=True
    )


def after(value, earlier):
    return lax.optimization_barrier((value, earlier))[0]


def on_device(tokens, weight, down, up, cotangent, sequence_index, storage_row):
    dp_count = lax.axis_size("dp")
    tensor_count = lax.axis_size("tensor")
    chips = tensor_count // 2
    me = lax.axis_index("dp")
    here = lax.axis_index("tensor")
    held, rank, block = down.shape
    out_block = up.shape[2]
    rows = tokens.shape[0]
    seqs = sequence_index.shape[0] // dp_count
    length = rows // seqs
    slots = dp_count
    width = block + out_block
    core = here & 1
    chip = here >> 1
    place = jnp.stack([me * seqs, core, chip, chip ^ 1]).astype(jnp.int32)
    pairs = [[t, t + 1] for t in range(0, tensor_count, 2)]
    same_core = [list(range(c, tensor_count, 2)) for c in range(2)]

    def shape(*dims, dtype=bf16):
        return jax.ShapeDtypeStruct(dims, dtype)

    def moved_along(value, distance):
        perm = [(t, (t + 2 * distance) % tensor_count) for t in range(tensor_count)]
        return lax.ppermute(value, "tensor", perm)

    spread = local_call(
        functools.partial(spread_body, held),
        shape(slots, length, width),
        [SMEM, SMEM, SMEM, VMEM, VMEM],
        moved=3 * slots * length * width,
        limit=HBM_LIMIT,
    )(place, sequence_index, storage_row, tokens, cotangent)
    arrived = exchange(spread, "dp")

    codes = jnp.arange(storage_row.shape[0], dtype=jnp.int32)
    matches = sequence_index[:, None] == codes[None, :]
    seq_rows = jnp.sum(jnp.where(matches, storage_row[None, :], 0), axis=1)
    local = seq_rows - held * me
    local = jnp.where((local >= 0) & (local < held), local, -1)
    pick = jnp.max(local.reshape(dp_count, seqs), axis=1).astype(jnp.int32)
    usage = jnp.sum((pick[:, None] == jnp.arange(held)[None, :]).astype(f32), axis=0)
    scale = adapter_scale / jnp.maximum(usage, 1.0)

    swap = [(t, t ^ 1) for t in range(tensor_count)]
    across = [(t, t ^ 2) for t in range(tensor_count)]
    quarter = chips // 2
    cot = after(cotangent, spread)
    opposite = moved_along(cot, quarter)
    near = local_call(
        pack_body,
        shape(quarter, rows, out_block),
        [VMEM] * quarter,
        moved=4 * quarter * rows * out_block,
    )(cot, moved_along(cot, -2), moved_along(cot, 2), opposite)
    far = lax.ppermute(near, "tensor", across)
    near_other = lax.ppermute(near, "tensor", swap)
    far_other = lax.ppermute(far, "tensor", swap)

    own, send = local_call(
        projection_body,
        (shape(chips, rows, out_block), shape(chips, rows, out_block)),
        [SMEM, VMEM, VMEM],
        flops=2 * rows * block * tensor_count * out_block,
        moved=2 * (rows * block + 2 * block * tensor_count * out_block),
    )(after(place, near), tokens, weight)
    came = lax.ppermute(send, "tensor", swap)
    arrived, near_other, far_other, own, came = lax.optimization_barrier(
        (arrived, near_other, far_other, own, came)
    )

    half = slots * length // 2
    part = local_call(
        rank_body,
        shape(slots * length, 2 * rank),
        [SMEM, VMEM, VMEM, VMEM],
        flops=2 * slots * length * width * held * rank,
        moved=2 * slots * length * width,
    )(pick, arrived, down, up)
    both = lax.all_gather(part, "tensor", axis_index_groups=pairs)
    mine = lax.dynamic_slice_in_dim(both, core * half, half, axis=1)
    mine = mine.astype(f32).sum(0).astype(bf16).reshape(chips, half // chips, 2 * rank)
    totals = local_call(
        total_body,
        shape(*mine.shape),
        [VMEM],
        moved=4 * half * 2 * rank,
    )(exchange(mine, "tensor", same_core))
    shared = exchange(totals, "tensor", same_core).reshape(half, 2 * rank)
    ranks = lax.all_gather(shared, "tensor", axis_index_groups=pairs).reshape(part.shape)

    masked = pltpu.VMEM((slots * length, held * rank), bf16)
    contributions = local_call(
        expand_body,
        shape(slots, length, width),
        [SMEM, VMEM, VMEM, VMEM],
        [masked, masked],
        flops=2 * slots * length * width * held * rank,
        moved=2 * slots * length * width,
    )(pick, ranks, down, up)
    returned = exchange(contributions, "dp")

    keep, give = local_call(
        pair_body,
        (shape(quarter, rows, out_block),) * 2,
        [VMEM, VMEM],
        moved=6 * chips * rows * out_block,
    )(after(own, contributions), came)
    crossed = lax.ppermute(give, "tensor", across)
    base = local_call(
        base_body,
        shape(rows, block, dtype=f32),
        [SMEM, VMEM, VMEM, VMEM, VMEM, VMEM],
        flops=2 * rows * block * tensor_count * out_block,
        moved=2 * (2 * rows * tensor_count * out_block),
    )(after(place, give), near, near_other, far, far_other, weight)
    summed = local_call(
        neighbour_body,
        (shape(rows, out_block),) * quarter,
        [VMEM, VMEM],
        moved=6 * quarter * rows * out_block,
    )(keep, crossed)
    opposite = moved_along(summed[3], quarter)
    parts = [summed[0], moved_along(summed[1], 2), moved_along(summed[2], -2), opposite]

    grad_down, grad_up = local_call(
        gradient_body,
        (shape(held, rank, block, dtype=f32), shape(held, rank, out_block, dtype=f32)),
        [SMEM, SMEM, VMEM, VMEM],
        [masked, masked],
        flops=2 * slots * length * width * held * rank,
        moved=2 * slots * length * width,
    )(pick, scale, ranks, arrived)
    token_gradient, key_value_output = local_call(
        functools.partial(final_body, held),
        (shape(rows, block), shape(rows, out_block)),
        [SMEM, SMEM, SMEM, VMEM, VMEM] + [VMEM] * quarter,
        moved=2 * (3 * rows * block + slots * length * width),
        limit=HBM_LIMIT,
    )(place, sequence_index, storage_row, base, returned, *parts)
    return (key_value_output, token_gradient, grad_down, grad_up)


def solution(mesh):
    in_specs = (
        P("dp", "tensor"),
        P("tensor", None),
        P("dp", None, "tensor"),
        P("dp", None, "tensor"),
        P("dp", "tensor"),
        P(),
        P(),
    )
    out_specs = (
        P("dp", "tensor"),
        P("dp", "tensor"),
        P("dp", None, "tensor"),
        P("dp", None, "tensor"),
    )
    return jax.shard_map(
        on_device, mesh=mesh, in_specs=in_specs, out_specs=out_specs, check_vma=False
    )
```

```python
import functools

import jax
import jax.numpy as jnp
from jax import lax
from jax.experimental import pallas as pl
from jax.experimental.pallas import tpu as pltpu
from jax.sharding import PartitionSpec as P

adapter_scale = 0.25
f32 = jnp.float32
bf16 = jnp.bfloat16
SMEM = pl.BlockSpec(memory_space=pltpu.SMEM)
VMEM = pl.BlockSpec(memory_space=pltpu.VMEM)
VMEM_LIMIT = 16 * 1024 * 1024
HBM_LIMIT = 60 * 1024 * 1024


def local_call(body, out_shape, specs, scratch=(), flops=0, moved=0, limit=VMEM_LIMIT):
    multiple = isinstance(out_shape, (tuple, list))
    return pl.pallas_call(
        body,
        out_shape=out_shape,
        in_specs=specs,
        out_specs=(VMEM,) * len(out_shape) if multiple else VMEM,
        scratch_shapes=list(scratch),
        compiler_params=pltpu.CompilerParams(vmem_limit_bytes=limit),
        cost_estimate=pl.CostEstimate(flops=flops, bytes_accessed=moved, transcendentals=0),
    )


def owner_of(place_ref, index_ref, storage_ref, held, j):
    return storage_ref[index_ref[place_ref[0] + j]] // held


def spread_body(held, place_ref, index_ref, storage_ref, tokens_ref, cot_ref, out_ref):
    slots, length, width = out_ref.shape
    block = tokens_ref.shape[1]
    out_ref[...] = jnp.zeros_like(out_ref)
    for j in range(tokens_ref.shape[0] // length):
        owner = owner_of(place_ref, index_ref, storage_ref, held, j)
        at = slice(j * length, (j + 1) * length)
        out_ref[owner, :, :block] = tokens_ref[at, :]
        out_ref[owner, :, block:] = cot_ref[at, :]


def chip_columns(place_ref, k, blocks, width):
    steps = (0, 2, blocks - 2, blocks // 2)
    chip = place_ref[2] if k < 4 else place_ref[3]
    chip = lax.rem(chip + steps[k % 4], blocks)
    return pl.ds(pl.multiple_of(chip * width, width), width)


def projection_body(place_ref, tokens_ref, weight_ref, own_ref, send_ref):
    blocks, rows, width = own_ref.shape
    core = place_ref[1]
    tokens = tokens_ref[...]
    for b in range(blocks):
        columns = chip_columns(place_ref, b, blocks, 2 * width)
        part = jnp.dot(tokens, weight_ref[:, columns], preferred_element_type=f32).astype(bf16)
        low, high = part[:, :width], part[:, width:]

        @pl.when(core == 0)
        def _():
            own_ref[b] = low
            send_ref[b] = high

        @pl.when(core != 0)
        def _():
            own_ref[b] = high
            send_ref[b] = low


def pair_body(own_ref, came_ref, *out_refs):
    count = len(out_refs)
    for k, out_ref in enumerate(out_refs):
        for b in range(2):
            at = k + b * count
            out_ref[b] = (own_ref[at].astype(f32) + came_ref[at].astype(f32)).astype(bf16)


def meet_body(*refs):
    part_refs, (mine_ref, other_ref) = refs[:-2], refs[-2:]
    for b, out_ref in enumerate((mine_ref, other_ref)):
        total = part_refs[0][b].astype(f32)
        for part_ref in part_refs[1:]:
            total = total + part_ref[b].astype(f32)
        out_ref[...] = total.astype(bf16)


def rank_body(pick_ref, rows_ref, down_ref, up_ref, out_ref):
    slots, length, width = rows_ref.shape
    held, rank, block = down_ref.shape
    flat = rows_ref[...].reshape(slots * length, width)
    dims = (((1,), (1,)), ((), ()))
    inner = [
        lax.dot_general(flat[:, :block], down_ref[a], dims, preferred_element_type=f32)
        for a in range(held)
    ]
    back = [
        lax.dot_general(flat[:, block:], up_ref[a], dims, preferred_element_type=f32)
        for a in range(held)
    ]
    joined = [jnp.concatenate([inner[a], back[a]], axis=1) for a in range(held)]
    for s in range(slots):
        at = slice(s * length, (s + 1) * length)
        value = jnp.zeros((length, 2 * rank), f32)
        for a in range(held):
            value = jnp.where(pick_ref[s] == a, joined[a][at], value)
        out_ref[at, :] = value.astype(bf16)


def total_body(parts_ref, out_ref):
    total = jnp.sum(parts_ref[...].astype(f32), axis=0).astype(bf16)
    for b in range(out_ref.shape[0]):
        out_ref[b] = total


def fill_masked(pick_ref, ranks_ref, masked_ref, left, slots, held, rank):
    length = ranks_ref.shape[0] // slots
    for s in range(slots):
        at = slice(s * length, (s + 1) * length)
        block = ranks_ref[at, :][:, left : left + rank]
        for a in range(held):
            masked_ref[at, a * rank : (a + 1) * rank] = jnp.where(
                pick_ref[s] == a, block, jnp.zeros_like(block)
            )


def expand_body(pick_ref, ranks_ref, down_ref, up_ref, out_ref, inner_ref, back_ref):
    slots, length, width = out_ref.shape
    held, rank, block = down_ref.shape
    fill_masked(pick_ref, ranks_ref, inner_ref, 0, slots, held, rank)
    fill_masked(pick_ref, ranks_ref, back_ref, rank, slots, held, rank)
    down = down_ref[...].reshape(held * rank, block)
    up = up_ref[...].reshape(held * rank, width - block)
    token_part = jnp.dot(back_ref[...], down, preferred_element_type=f32) * adapter_scale
    output_part = jnp.dot(inner_ref[...], up, preferred_element_type=f32) * adapter_scale
    out_ref[:, :, :block] = token_part.astype(bf16).reshape(slots, length, block)
    out_ref[:, :, block:] = output_part.astype(bf16).reshape(slots, length, width - block)


def gradient_body(
    pick_ref, scale_ref, ranks_ref, rows_ref, down_out_ref, up_out_ref, inner_ref, back_ref
):
    slots, length, width = rows_ref.shape
    held, rank, block = down_out_ref.shape
    fill_masked(pick_ref, ranks_ref, inner_ref, 0, slots, held, rank)
    fill_masked(pick_ref, ranks_ref, back_ref, rank, slots, held, rank)
    flat = rows_ref[...].reshape(slots * length, width)
    dims = (((0,), (0,)), ((), ()))
    down = lax.dot_general(back_ref[...], flat[:, :block], dims, preferred_element_type=f32)
    up = lax.dot_general(inner_ref[...], flat[:, block:], dims, preferred_element_type=f32)
    for a in range(held):
        at = slice(a * rank, (a + 1) * rank)
        down_out_ref[a] = down[at] * scale_ref[a]
        up_out_ref[a] = up[at] * scale_ref[a]


def base_body(place_ref, near_ref, near_other_ref, far_ref, far_other_ref, weight_ref, out_ref):
    blocks, rows, width = near_ref.shape
    dims = (((1,), (1,)), ((), ()))
    first_core = place_ref[1] == 0
    for k in range(2 * blocks):
        own_ref, other_ref = (near_ref, near_other_ref) if k < blocks else (far_ref, far_other_ref)
        own, other = own_ref[k % blocks], other_ref[k % blocks]
        low = jnp.where(first_core, own, other)
        high = jnp.where(first_core, other, own)
        pair = jnp.concatenate([low, high], axis=1)
        odd = lax.rem(place_ref[2] + k // blocks, 2)
        chip = 2 * (k % blocks) + odd
        columns = pl.ds(pl.multiple_of(chip * 2 * width, 2 * width), 2 * width)
        part = lax.dot_general(pair, weight_ref[:, columns], dims, preferred_element_type=f32)
        out_ref[...] = part if k == 0 else out_ref[...] + part


def final_body(held, place_ref, index_ref, storage_ref, base_ref, came_ref, *refs):
    part_refs, (token_out_ref, output_ref) = refs[:-2], refs[-2:]
    slots, length, width = came_ref.shape
    block = base_ref.shape[1]
    for j in range(base_ref.shape[0] // length):
        owner = owner_of(place_ref, index_ref, storage_ref, held, j)
        at = slice(j * length, (j + 1) * length)
        came = came_ref[owner].astype(f32)
        token_out_ref[at, :] = (base_ref[at, :] + came[:, :block]).astype(bf16)
        total = came[:, block:]
        for part_ref in part_refs:
            total = total + part_ref[at, :].astype(f32)
        output_ref[at, :] = total.astype(bf16)


def exchange(value, axis, groups=None):
    return lax.all_to_all(
        value, axis, split_axis=0, concat_axis=0, axis_index_groups=groups, tiled=True
    )


def after(value, earlier):
    return lax.optimization_barrier((value, earlier))[0]


def on_device(tokens, weight, down, up, cotangent, sequence_index, storage_row):
    dp_count = lax.axis_size("dp")
    tensor_count = lax.axis_size("tensor")
    chips = tensor_count // 2
    me = lax.axis_index("dp")
    here = lax.axis_index("tensor")
    held, rank, block = down.shape
    out_block = up.shape[2]
    rows = tokens.shape[0]
    seqs = sequence_index.shape[0] // dp_count
    length = rows // seqs
    slots = dp_count
    width = block + out_block
    core = here & 1
    chip = here >> 1
    place = jnp.stack([me * seqs, core, chip, chip ^ 1]).astype(jnp.int32)
    pairs = [[t, t + 1] for t in range(0, tensor_count, 2)]
    same_core = [list(range(c, tensor_count, 2)) for c in range(2)]

    def shape(*dims, dtype=bf16):
        return jax.ShapeDtypeStruct(dims, dtype)

    def moved_along(value, distance):
        perm = [(t, (t + 2 * distance) % tensor_count) for t in range(tensor_count)]
        return lax.ppermute(value, "tensor", perm)

    spread = local_call(
        functools.partial(spread_body, held),
        shape(slots, length, width),
        [SMEM, SMEM, SMEM, VMEM, VMEM],
        moved=3 * slots * length * width,
        limit=HBM_LIMIT,
    )(place, sequence_index, storage_row, tokens, cotangent)
    arrived = exchange(spread, "dp")

    codes = jnp.arange(storage_row.shape[0], dtype=jnp.int32)
    matches = sequence_index[:, None] == codes[None, :]
    seq_rows = jnp.sum(jnp.where(matches, storage_row[None, :], 0), axis=1)
    local = seq_rows - held * me
    local = jnp.where((local >= 0) & (local < held), local, -1)
    pick = jnp.max(local.reshape(dp_count, seqs), axis=1).astype(jnp.int32)
    usage = jnp.sum((pick[:, None] == jnp.arange(held)[None, :]).astype(f32), axis=0)
    scale = adapter_scale / jnp.maximum(usage, 1.0)

    swap = [(t, t ^ 1) for t in range(tensor_count)]
    across = [(t, t ^ 2) for t in range(tensor_count)]
    quarter = chips // 2
    alternate = [list(range(p, tensor_count, 4)) for p in range(4)]
    near = lax.all_gather(after(cotangent, spread), "tensor", axis_index_groups=alternate)
    far = lax.ppermute(near, "tensor", across)
    near_other = lax.ppermute(near, "tensor", swap)
    far_other = lax.ppermute(far, "tensor", swap)

    own, send = local_call(
        projection_body,
        (shape(chips, rows, out_block), shape(chips, rows, out_block)),
        [SMEM, VMEM, VMEM],
        flops=2 * rows * block * tensor_count * out_block,
        moved=2 * (rows * block + 2 * block * tensor_count * out_block),
    )(after(place, near), tokens, weight)
    came = lax.ppermute(send, "tensor", swap)
    arrived, near_other, far_other, own, came = lax.optimization_barrier(
        (arrived, near_other, far_other, own, came)
    )

    half = slots * length // 2
    part = local_call(
        rank_body,
        shape(slots * length, 2 * rank),
        [SMEM, VMEM, VMEM, VMEM],
        flops=2 * slots * length * width * held * rank,
        moved=2 * slots * length * width,
    )(pick, arrived, down, up)
    both = lax.all_gather(part, "tensor", axis_index_groups=pairs)
    mine = lax.dynamic_slice_in_dim(both, core * half, half, axis=1)
    mine = mine.astype(f32).sum(0).astype(bf16).reshape(chips, half // chips, 2 * rank)
    totals = local_call(
        total_body,
        shape(*mine.shape),
        [VMEM],
        moved=4 * half * 2 * rank,
    )(exchange(mine, "tensor", same_core))
    shared = exchange(totals, "tensor", same_core).reshape(half, 2 * rank)
    ranks = lax.all_gather(shared, "tensor", axis_index_groups=pairs).reshape(part.shape)

    masked = pltpu.VMEM((slots * length, held * rank), bf16)
    contributions = local_call(
        expand_body,
        shape(slots, length, width),
        [SMEM, VMEM, VMEM, VMEM],
        [masked, masked],
        flops=2 * slots * length * width * held * rank,
        moved=2 * slots * length * width,
    )(pick, ranks, down, up)
    returned = exchange(contributions, "dp")

    paired = local_call(
        pair_body,
        (shape(2, rows, out_block),) * quarter,
        [VMEM, VMEM],
        moved=6 * chips * rows * out_block,
    )(after(own, contributions), came)
    sums = [paired[0], moved_along(paired[3], quarter)]
    sums += [moved_along(paired[1], 2), moved_along(paired[2], -2)]
    base = local_call(
        base_body,
        shape(rows, block, dtype=f32),
        [SMEM, VMEM, VMEM, VMEM, VMEM, VMEM],
        flops=2 * rows * block * tensor_count * out_block,
        moved=2 * (2 * rows * tensor_count * out_block),
    )(after(place, paired[0]), near, near_other, far, far_other, weight)
    grad_down, grad_up = local_call(
        gradient_body,
        (shape(held, rank, block, dtype=f32), shape(held, rank, out_block, dtype=f32)),
        [SMEM, SMEM, VMEM, VMEM],
        [masked, masked],
        flops=2 * slots * length * width * held * rank,
        moved=2 * slots * length * width,
    )(pick, scale, ranks, arrived)
    sums, base, grad_down, grad_up = lax.optimization_barrier((sums, base, grad_down, grad_up))
    mine_sum, other_sum = local_call(
        meet_body,
        (shape(rows, out_block),) * 2,
        [VMEM] * quarter,
        moved=2 * 10 * rows * out_block,
    )(*sums)
    parts = [mine_sum, lax.ppermute(other_sum, "tensor", across)]

    token_gradient, key_value_output = local_call(
        functools.partial(final_body, held),
        (shape(rows, block), shape(rows, out_block)),
        [SMEM, SMEM, SMEM, VMEM, VMEM, VMEM, VMEM],
        moved=2 * (3 * rows * block + slots * length * width),
    )(place, sequence_index, storage_row, base, returned, *parts)
    return (key_value_output, token_gradient, grad_down, grad_up)


def solution(mesh):
    in_specs = (
        P("dp", "tensor"),
        P("tensor", None),
        P("dp", None, "tensor"),
        P("dp", None, "tensor"),
        P("dp", "tensor"),
        P(),
        P(),
    )
    out_specs = (
        P("dp", "tensor"),
        P("dp", "tensor"),
        P("dp", None, "tensor"),
        P("dp", None, "tensor"),
    )
    return jax.shard_map(
        on_device, mesh=mesh, in_specs=in_specs, out_specs=out_specs, check_vma=False
    )
```

```python
import functools

import jax
import jax.numpy as jnp
from jax import lax
from jax.experimental import pallas as pl
from jax.experimental.pallas import tpu as pltpu
from jax.sharding import PartitionSpec as P

adapter_scale = 0.25
f32 = jnp.float32
bf16 = jnp.bfloat16
SMEM = pl.BlockSpec(memory_space=pltpu.SMEM)
VMEM = pl.BlockSpec(memory_space=pltpu.VMEM)
VMEM_LIMIT = 16 * 1024 * 1024
HBM_LIMIT = 60 * 1024 * 1024


def local_call(body, out_shape, specs, scratch=(), flops=0, moved=0, limit=VMEM_LIMIT):
    multiple = isinstance(out_shape, (tuple, list))
    return pl.pallas_call(
        body,
        out_shape=out_shape,
        in_specs=specs,
        out_specs=(VMEM,) * len(out_shape) if multiple else VMEM,
        scratch_shapes=list(scratch),
        compiler_params=pltpu.CompilerParams(vmem_limit_bytes=limit),
        cost_estimate=pl.CostEstimate(flops=flops, bytes_accessed=moved, transcendentals=0),
    )


def owner_of(place_ref, index_ref, storage_ref, held, j):
    return storage_ref[index_ref[place_ref[0] + j]] // held


def spread_body(held, place_ref, index_ref, storage_ref, tokens_ref, cot_ref, out_ref):
    slots, length, width = out_ref.shape
    block = tokens_ref.shape[1]
    out_ref[...] = jnp.zeros_like(out_ref)
    for j in range(tokens_ref.shape[0] // length):
        owner = owner_of(place_ref, index_ref, storage_ref, held, j)
        at = slice(j * length, (j + 1) * length)
        out_ref[owner, :, :block] = tokens_ref[at, :]
        out_ref[owner, :, block:] = cot_ref[at, :]


def chip_columns(place_ref, k, blocks, width):
    steps = (0, 2, blocks - 2, blocks // 2)
    chip = place_ref[2] if k < 4 else place_ref[3]
    chip = lax.rem(chip + steps[k % 4], blocks)
    return pl.ds(pl.multiple_of(chip * width, width), width)


def projection_body(place_ref, tokens_ref, weight_ref, own_ref, send_ref):
    blocks, rows, width = own_ref.shape
    core = place_ref[1]
    tokens = tokens_ref[...]
    for b in range(blocks):
        columns = chip_columns(place_ref, b, blocks, 2 * width)
        part = jnp.dot(tokens, weight_ref[:, columns], preferred_element_type=f32).astype(bf16)
        low, high = part[:, :width], part[:, width:]

        @pl.when(core == 0)
        def _():
            own_ref[b] = low
            send_ref[b] = high

        @pl.when(core != 0)
        def _():
            own_ref[b] = high
            send_ref[b] = low


def pair_body(own_ref, came_ref, keep_ref, give_ref):
    half = keep_ref.shape[0]
    for b in range(half):
        keep_ref[b] = (own_ref[b].astype(f32) + came_ref[b].astype(f32)).astype(bf16)
        other = own_ref[half + b].astype(f32) + came_ref[half + b].astype(f32)
        give_ref[b] = other.astype(bf16)


def neighbour_body(keep_ref, came_ref, *out_refs):
    for b, out_ref in enumerate(out_refs):
        out_ref[...] = (keep_ref[b].astype(f32) + came_ref[b].astype(f32)).astype(bf16)


def rank_body(pick_ref, rows_ref, down_ref, up_ref, out_ref):
    slots, length, width = rows_ref.shape
    held, rank, block = down_ref.shape
    flat = rows_ref[...].reshape(slots * length, width)
    dims = (((1,), (1,)), ((), ()))
    inner = [
        lax.dot_general(flat[:, :block], down_ref[a], dims, preferred_element_type=f32)
        for a in range(held)
    ]
    back = [
        lax.dot_general(flat[:, block:], up_ref[a], dims, preferred_element_type=f32)
        for a in range(held)
    ]
    joined = [jnp.concatenate([inner[a], back[a]], axis=1) for a in range(held)]
    for s in range(slots):
        at = slice(s * length, (s + 1) * length)
        value = jnp.zeros((length, 2 * rank), f32)
        for a in range(held):
            value = jnp.where(pick_ref[s] == a, joined[a][at], value)
        out_ref[at, :] = value.astype(bf16)


def total_body(parts_ref, out_ref):
    total = jnp.sum(parts_ref[...].astype(f32), axis=0).astype(bf16)
    for b in range(out_ref.shape[0]):
        out_ref[b] = total


def fill_masked(pick_ref, ranks_ref, masked_ref, left, slots, held, rank):
    length = ranks_ref.shape[0] // slots
    for s in range(slots):
        at = slice(s * length, (s + 1) * length)
        block = ranks_ref[at, :][:, left : left + rank]
        for a in range(held):
            masked_ref[at, a * rank : (a + 1) * rank] = jnp.where(
                pick_ref[s] == a, block, jnp.zeros_like(block)
            )


def expand_body(pick_ref, ranks_ref, down_ref, up_ref, out_ref, inner_ref, back_ref):
    slots, length, width = out_ref.shape
    held, rank, block = down_ref.shape
    fill_masked(pick_ref, ranks_ref, inner_ref, 0, slots, held, rank)
    fill_masked(pick_ref, ranks_ref, back_ref, rank, slots, held, rank)
    down = down_ref[...].reshape(held * rank, block)
    up = up_ref[...].reshape(held * rank, width - block)
    token_part = jnp.dot(back_ref[...], down, preferred_element_type=f32) * adapter_scale
    output_part = jnp.dot(inner_ref[...], up, preferred_element_type=f32) * adapter_scale
    out_ref[:, :, :block] = token_part.astype(bf16).reshape(slots, length, block)
    out_ref[:, :, block:] = output_part.astype(bf16).reshape(slots, length, width - block)


def gradient_body(
    pick_ref, scale_ref, ranks_ref, rows_ref, down_out_ref, up_out_ref, inner_ref, back_ref
):
    slots, length, width = rows_ref.shape
    held, rank, block = down_out_ref.shape
    fill_masked(pick_ref, ranks_ref, inner_ref, 0, slots, held, rank)
    fill_masked(pick_ref, ranks_ref, back_ref, rank, slots, held, rank)
    flat = rows_ref[...].reshape(slots * length, width)
    dims = (((0,), (0,)), ((), ()))
    down = lax.dot_general(back_ref[...], flat[:, :block], dims, preferred_element_type=f32)
    up = lax.dot_general(inner_ref[...], flat[:, block:], dims, preferred_element_type=f32)
    for a in range(held):
        at = slice(a * rank, (a + 1) * rank)
        down_out_ref[a] = down[at] * scale_ref[a]
        up_out_ref[a] = up[at] * scale_ref[a]


def base_body(place_ref, near_ref, near_other_ref, far_ref, far_other_ref, weight_ref, out_ref):
    blocks, rows, width = near_ref.shape
    dims = (((1,), (1,)), ((), ()))
    first_core = place_ref[1] == 0
    for k in range(2 * blocks):
        own_ref, other_ref = (near_ref, near_other_ref) if k < blocks else (far_ref, far_other_ref)
        own, other = own_ref[k % blocks], other_ref[k % blocks]
        low = jnp.where(first_core, own, other)
        high = jnp.where(first_core, other, own)
        pair = jnp.concatenate([low, high], axis=1)
        odd = lax.rem(place_ref[2] + k // blocks, 2)
        chip = 2 * (k % blocks) + odd
        columns = pl.ds(pl.multiple_of(chip * 2 * width, 2 * width), 2 * width)
        part = lax.dot_general(pair, weight_ref[:, columns], dims, preferred_element_type=f32)
        out_ref[...] = part if k == 0 else out_ref[...] + part


def final_body(held, place_ref, index_ref, storage_ref, base_ref, came_ref, *refs):
    part_refs, (token_out_ref, output_ref) = refs[:-2], refs[-2:]
    slots, length, width = came_ref.shape
    block = base_ref.shape[1]
    for j in range(base_ref.shape[0] // length):
        owner = owner_of(place_ref, index_ref, storage_ref, held, j)
        at = slice(j * length, (j + 1) * length)
        came = came_ref[owner].astype(f32)
        token_out_ref[at, :] = (base_ref[at, :] + came[:, :block]).astype(bf16)
        total = came[:, block:]
        for part_ref in part_refs:
            total = total + part_ref[at, :].astype(f32)
        output_ref[at, :] = total.astype(bf16)


def exchange(value, axis, groups=None):
    return lax.all_to_all(
        value, axis, split_axis=0, concat_axis=0, axis_index_groups=groups, tiled=True
    )


def after(value, earlier):
    return lax.optimization_barrier((value, earlier))[0]


def on_device(tokens, weight, down, up, cotangent, sequence_index, storage_row):
    dp_count = lax.axis_size("dp")
    tensor_count = lax.axis_size("tensor")
    chips = tensor_count // 2
    me = lax.axis_index("dp")
    here = lax.axis_index("tensor")
    held, rank, block = down.shape
    out_block = up.shape[2]
    rows = tokens.shape[0]
    seqs = sequence_index.shape[0] // dp_count
    length = rows // seqs
    slots = dp_count
    width = block + out_block
    core = here & 1
    chip = here >> 1
    place = jnp.stack([me * seqs, core, chip, chip ^ 1]).astype(jnp.int32)
    pairs = [[t, t + 1] for t in range(0, tensor_count, 2)]
    same_core = [list(range(c, tensor_count, 2)) for c in range(2)]

    def shape(*dims, dtype=bf16):
        return jax.ShapeDtypeStruct(dims, dtype)

    def moved_along(value, distance):
        perm = [(t, (t + 2 * distance) % tensor_count) for t in range(tensor_count)]
        return lax.ppermute(value, "tensor", perm)

    spread = local_call(
        functools.partial(spread_body, held),
        shape(slots, length, width),
        [SMEM, SMEM, SMEM, VMEM, VMEM],
        moved=3 * slots * length * width,
        limit=HBM_LIMIT,
    )(place, sequence_index, storage_row, tokens, cotangent)
    arrived = exchange(spread, "dp")

    codes = jnp.arange(storage_row.shape[0], dtype=jnp.int32)
    matches = sequence_index[:, None] == codes[None, :]
    seq_rows = jnp.sum(jnp.where(matches, storage_row[None, :], 0), axis=1)
    local = seq_rows - held * me
    local = jnp.where((local >= 0) & (local < held), local, -1)
    pick = jnp.max(local.reshape(dp_count, seqs), axis=1).astype(jnp.int32)
    usage = jnp.sum((pick[:, None] == jnp.arange(held)[None, :]).astype(f32), axis=0)
    scale = adapter_scale / jnp.maximum(usage, 1.0)

    swap = [(t, t ^ 1) for t in range(tensor_count)]
    across = [(t, t ^ 2) for t in range(tensor_count)]
    quarter = chips // 2
    alternate = [list(range(p, tensor_count, 4)) for p in range(4)]
    near = lax.all_gather(after(cotangent, spread), "tensor", axis_index_groups=alternate)
    far = lax.ppermute(near, "tensor", across)

    own, send = local_call(
        projection_body,
        (shape(chips, rows, out_block), shape(chips, rows, out_block)),
        [SMEM, VMEM, VMEM],
        flops=2 * rows * block * tensor_count * out_block,
        moved=2 * (rows * block + 2 * block * tensor_count * out_block),
    )(after(place, near), tokens, weight)
    arrived, far, own, send = lax.optimization_barrier((arrived, far, own, send))
    came = lax.ppermute(send, "tensor", swap)

    half = slots * length // 2
    part = local_call(
        rank_body,
        shape(slots * length, 2 * rank),
        [SMEM, VMEM, VMEM, VMEM],
        flops=2 * slots * length * width * held * rank,
        moved=2 * slots * length * width,
    )(pick, arrived, down, up)
    both = lax.all_gather(part, "tensor", axis_index_groups=pairs)
    mine = lax.dynamic_slice_in_dim(both, core * half, half, axis=1)
    mine = mine.astype(f32).sum(0).astype(bf16).reshape(chips, half // chips, 2 * rank)
    pieces, came = lax.optimization_barrier((exchange(mine, "tensor", same_core), came))
    totals = local_call(
        total_body,
        shape(*mine.shape),
        [VMEM],
        moved=4 * half * 2 * rank,
    )(pieces)
    shared = exchange(totals, "tensor", same_core).reshape(half, 2 * rank)
    ranks = lax.all_gather(shared, "tensor", axis_index_groups=pairs).reshape(part.shape)

    masked = pltpu.VMEM((slots * length, held * rank), bf16)
    contributions = local_call(
        expand_body,
        shape(slots, length, width),
        [SMEM, VMEM, VMEM, VMEM],
        [masked, masked],
        flops=2 * slots * length * width * held * rank,
        moved=2 * slots * length * width,
    )(pick, ranks, down, up)
    returned = exchange(contributions, "dp")

    keep, give = local_call(
        pair_body,
        (shape(quarter, rows, out_block),) * 2,
        [VMEM, VMEM],
        moved=6 * chips * rows * out_block,
    )(after(own, contributions), came)
    far_other = lax.ppermute(after(far, give), "tensor", swap)
    near_other = lax.ppermute(after(near, give), "tensor", swap)
    crossed = lax.ppermute(give, "tensor", across)
    grad_down, grad_up = local_call(
        gradient_body,
        (shape(held, rank, block, dtype=f32), shape(held, rank, out_block, dtype=f32)),
        [SMEM, SMEM, VMEM, VMEM],
        [masked, masked],
        flops=2 * slots * length * width * held * rank,
        moved=2 * slots * length * width,
    )(pick, after(scale, give), ranks, arrived)
    base = local_call(
        base_body,
        shape(rows, block, dtype=f32),
        [SMEM, VMEM, VMEM, VMEM, VMEM, VMEM],
        flops=2 * rows * block * tensor_count * out_block,
        moved=2 * (2 * rows * tensor_count * out_block),
    )(after(place, give), near, near_other, far, far_other, weight)
    crossed, keep, base, grad_down, grad_up = lax.optimization_barrier(
        (crossed, keep, base, grad_down, grad_up)
    )
    summed = local_call(
        neighbour_body,
        (shape(rows, out_block),) * quarter,
        [VMEM, VMEM],
        moved=6 * quarter * rows * out_block,
    )(keep, crossed)
    parts = [summed[0], moved_along(summed[3], quarter)]
    parts += [moved_along(summed[1], 2), moved_along(summed[2], -2)]

    token_gradient, key_value_output = local_call(
        functools.partial(final_body, held),
        (shape(rows, block), shape(rows, out_block)),
        [SMEM, SMEM, SMEM, VMEM, VMEM] + [VMEM] * quarter,
        moved=2 * (3 * rows * block + slots * length * width),
    )(place, sequence_index, storage_row, base, returned, *parts)
    return (key_value_output, token_gradient, grad_down, grad_up)


def solution(mesh):
    in_specs = (
        P("dp", "tensor"),
        P("tensor", None),
        P("dp", None, "tensor"),
        P("dp", None, "tensor"),
        P("dp", "tensor"),
        P(),
        P(),
    )
    out_specs = (
        P("dp", "tensor"),
        P("dp", "tensor"),
        P("dp", None, "tensor"),
        P("dp", None, "tensor"),
    )
    return jax.shard_map(
        on_device, mesh=mesh, in_specs=in_specs, out_specs=out_specs, check_vma=False
    )
```

```python
import functools

import jax
import jax.numpy as jnp
from jax import lax
from jax.experimental import pallas as pl
from jax.experimental.pallas import tpu as pltpu
from jax.sharding import PartitionSpec as P

adapter_scale = 0.25
f32 = jnp.float32
bf16 = jnp.bfloat16
SMEM = pl.BlockSpec(memory_space=pltpu.SMEM)
VMEM = pl.BlockSpec(memory_space=pltpu.VMEM)
VMEM_LIMIT = 16 * 1024 * 1024
HBM_LIMIT = 60 * 1024 * 1024


def local_call(body, out_shape, specs, scratch=(), flops=0, moved=0, limit=VMEM_LIMIT):
    multiple = isinstance(out_shape, (tuple, list))
    return pl.pallas_call(
        body,
        out_shape=out_shape,
        in_specs=specs,
        out_specs=(VMEM,) * len(out_shape) if multiple else VMEM,
        scratch_shapes=list(scratch),
        compiler_params=pltpu.CompilerParams(vmem_limit_bytes=limit),
        cost_estimate=pl.CostEstimate(flops=flops, bytes_accessed=moved, transcendentals=0),
    )


def owner_of(place_ref, index_ref, storage_ref, held, j):
    return storage_ref[index_ref[place_ref[0] + j]] // held


def spread_body(held, place_ref, index_ref, storage_ref, tokens_ref, cot_ref, out_ref):
    slots, length, width = out_ref.shape
    block = tokens_ref.shape[1]
    out_ref[...] = jnp.zeros_like(out_ref)
    for j in range(tokens_ref.shape[0] // length):
        owner = owner_of(place_ref, index_ref, storage_ref, held, j)
        at = slice(j * length, (j + 1) * length)
        out_ref[owner, :, :block] = tokens_ref[at, :]
        out_ref[owner, :, block:] = cot_ref[at, :]


def chip_columns(place_ref, k, blocks, width):
    steps = (0, 2, blocks - 2, blocks // 2)
    chip = place_ref[2] if k < 4 else place_ref[3]
    chip = lax.rem(chip + steps[k % 4], blocks)
    return pl.ds(pl.multiple_of(chip * width, width), width)


def projection_body(place_ref, tokens_ref, weight_ref, own_ref, send_ref):
    blocks, rows, width = own_ref.shape
    core = place_ref[1]
    tokens = tokens_ref[...]
    for b in range(blocks):
        columns = chip_columns(place_ref, b, blocks, 2 * width)
        part = jnp.dot(tokens, weight_ref[:, columns], preferred_element_type=f32).astype(bf16)
        low, high = part[:, :width], part[:, width:]

        @pl.when(core == 0)
        def _():
            own_ref[b] = low
            send_ref[b] = high

        @pl.when(core != 0)
        def _():
            own_ref[b] = high
            send_ref[b] = low


def pair_body(own_ref, came_ref, keep_ref, give_ref):
    half = keep_ref.shape[0]
    for b in range(half):
        keep_ref[b] = (own_ref[b].astype(f32) + came_ref[b].astype(f32)).astype(bf16)
        other = own_ref[half + b].astype(f32) + came_ref[half + b].astype(f32)
        give_ref[b] = other.astype(bf16)


def neighbour_body(keep_ref, came_ref, *out_refs):
    for b, out_ref in enumerate(out_refs):
        out_ref[...] = (keep_ref[b].astype(f32) + came_ref[b].astype(f32)).astype(bf16)


def rank_body(pick_ref, rows_ref, down_ref, up_ref, out_ref):
    slots, length, width = rows_ref.shape
    held, rank, block = down_ref.shape
    flat = rows_ref[...].reshape(slots * length, width)
    dims = (((1,), (1,)), ((), ()))
    inner = [
        lax.dot_general(flat[:, :block], down_ref[a], dims, preferred_element_type=f32)
        for a in range(held)
    ]
    back = [
        lax.dot_general(flat[:, block:], up_ref[a], dims, preferred_element_type=f32)
        for a in range(held)
    ]
    joined = [jnp.concatenate([inner[a], back[a]], axis=1) for a in range(held)]
    for s in range(slots):
        at = slice(s * length, (s + 1) * length)
        value = jnp.zeros((length, 2 * rank), f32)
        for a in range(held):
            value = jnp.where(pick_ref[s] == a, joined[a][at], value)
        out_ref[at, :] = value.astype(bf16)


def total_body(parts_ref, out_ref):
    total = jnp.sum(parts_ref[...].astype(f32), axis=0).astype(bf16)
    for b in range(out_ref.shape[0]):
        out_ref[b] = total


def fill_masked(pick_ref, ranks_ref, masked_ref, left, slots, held, rank):
    length = ranks_ref.shape[0] // slots
    for s in range(slots):
        at = slice(s * length, (s + 1) * length)
        block = ranks_ref[at, :][:, left : left + rank]
        for a in range(held):
            masked_ref[at, a * rank : (a + 1) * rank] = jnp.where(
                pick_ref[s] == a, block, jnp.zeros_like(block)
            )


def expand_body(pick_ref, ranks_ref, down_ref, up_ref, out_ref, inner_ref, back_ref):
    slots, length, width = out_ref.shape
    held, rank, block = down_ref.shape
    fill_masked(pick_ref, ranks_ref, inner_ref, 0, slots, held, rank)
    fill_masked(pick_ref, ranks_ref, back_ref, rank, slots, held, rank)
    down = down_ref[...].reshape(held * rank, block)
    up = up_ref[...].reshape(held * rank, width - block)
    token_part = jnp.dot(back_ref[...], down, preferred_element_type=f32) * adapter_scale
    output_part = jnp.dot(inner_ref[...], up, preferred_element_type=f32) * adapter_scale
    out_ref[:, :, :block] = token_part.astype(bf16).reshape(slots, length, block)
    out_ref[:, :, block:] = output_part.astype(bf16).reshape(slots, length, width - block)


def gradient_body(
    pick_ref, scale_ref, ranks_ref, rows_ref, down_out_ref, up_out_ref, inner_ref, back_ref
):
    slots, length, width = rows_ref.shape
    held, rank, block = down_out_ref.shape
    fill_masked(pick_ref, ranks_ref, inner_ref, 0, slots, held, rank)
    fill_masked(pick_ref, ranks_ref, back_ref, rank, slots, held, rank)
    flat = rows_ref[...].reshape(slots * length, width)
    dims = (((0,), (0,)), ((), ()))
    down = lax.dot_general(back_ref[...], flat[:, :block], dims, preferred_element_type=f32)
    up = lax.dot_general(inner_ref[...], flat[:, block:], dims, preferred_element_type=f32)
    for a in range(held):
        at = slice(a * rank, (a + 1) * rank)
        down_out_ref[a] = down[at] * scale_ref[a]
        up_out_ref[a] = up[at] * scale_ref[a]


def base_body(place_ref, near_ref, near_other_ref, far_ref, far_other_ref, weight_ref, out_ref):
    blocks, rows, width = near_ref.shape
    dims = (((1,), (1,)), ((), ()))
    first_core = place_ref[1] == 0
    for k in range(2 * blocks):
        own_ref, other_ref = (near_ref, near_other_ref) if k < blocks else (far_ref, far_other_ref)
        own, other = own_ref[k % blocks], other_ref[k % blocks]
        low = jnp.where(first_core, own, other)
        high = jnp.where(first_core, other, own)
        pair = jnp.concatenate([low, high], axis=1)
        odd = lax.rem(place_ref[2] + k // blocks, 2)
        chip = 2 * (k % blocks) + odd
        columns = pl.ds(pl.multiple_of(chip * 2 * width, 2 * width), 2 * width)
        part = lax.dot_general(pair, weight_ref[:, columns], dims, preferred_element_type=f32)
        out_ref[...] = part if k == 0 else out_ref[...] + part


def final_body(held, place_ref, index_ref, storage_ref, base_ref, came_ref, *refs):
    part_refs, (token_out_ref, output_ref) = refs[:-2], refs[-2:]
    slots, length, width = came_ref.shape
    block = base_ref.shape[1]
    for j in range(base_ref.shape[0] // length):
        owner = owner_of(place_ref, index_ref, storage_ref, held, j)
        at = slice(j * length, (j + 1) * length)
        came = came_ref[owner].astype(f32)
        token_out_ref[at, :] = (base_ref[at, :] + came[:, :block]).astype(bf16)
        total = came[:, block:]
        for part_ref in part_refs:
            total = total + part_ref[at, :].astype(f32)
        output_ref[at, :] = total.astype(bf16)


def exchange(value, axis, groups=None):
    return lax.all_to_all(
        value, axis, split_axis=0, concat_axis=0, axis_index_groups=groups, tiled=True
    )


def after(value, earlier):
    return lax.optimization_barrier((value, earlier))[0]


def on_device(tokens, weight, down, up, cotangent, sequence_index, storage_row):
    dp_count = lax.axis_size("dp")
    tensor_count = lax.axis_size("tensor")
    chips = tensor_count // 2
    me = lax.axis_index("dp")
    here = lax.axis_index("tensor")
    held, rank, block = down.shape
    out_block = up.shape[2]
    rows = tokens.shape[0]
    seqs = sequence_index.shape[0] // dp_count
    length = rows // seqs
    slots = dp_count
    width = block + out_block
    core = here & 1
    chip = here >> 1
    place = jnp.stack([me * seqs, core, chip, chip ^ 1]).astype(jnp.int32)
    pairs = [[t, t + 1] for t in range(0, tensor_count, 2)]
    same_core = [list(range(c, tensor_count, 2)) for c in range(2)]

    def shape(*dims, dtype=bf16):
        return jax.ShapeDtypeStruct(dims, dtype)

    def moved_along(value, distance):
        perm = [(t, (t + 2 * distance) % tensor_count) for t in range(tensor_count)]
        return lax.ppermute(value, "tensor", perm)

    spread = local_call(
        functools.partial(spread_body, held),
        shape(slots, length, width),
        [SMEM, SMEM, SMEM, VMEM, VMEM],
        moved=3 * slots * length * width,
        limit=HBM_LIMIT,
    )(place, sequence_index, storage_row, tokens, cotangent)
    arrived = exchange(spread, "dp")

    codes = jnp.arange(storage_row.shape[0], dtype=jnp.int32)
    matches = sequence_index[:, None] == codes[None, :]
    seq_rows = jnp.sum(jnp.where(matches, storage_row[None, :], 0), axis=1)
    local = seq_rows - held * me
    local = jnp.where((local >= 0) & (local < held), local, -1)
    pick = jnp.max(local.reshape(dp_count, seqs), axis=1).astype(jnp.int32)
    usage = jnp.sum((pick[:, None] == jnp.arange(held)[None, :]).astype(f32), axis=0)
    scale = adapter_scale / jnp.maximum(usage, 1.0)

    swap = [(t, t ^ 1) for t in range(tensor_count)]
    across = [(t, t ^ 2) for t in range(tensor_count)]
    quarter = chips // 2
    alternate = [list(range(p, tensor_count, 4)) for p in range(4)]
    near = lax.all_gather(after(cotangent, spread), "tensor", axis_index_groups=alternate)
    far = lax.ppermute(near, "tensor", across)

    own, send = local_call(
        projection_body,
        (shape(chips, rows, out_block), shape(chips, rows, out_block)),
        [SMEM, VMEM, VMEM],
        flops=2 * rows * block * tensor_count * out_block,
        moved=2 * (rows * block + 2 * block * tensor_count * out_block),
    )(after(place, near), tokens, weight)
    arrived, far, own, send = lax.optimization_barrier((arrived, far, own, send))
    came = lax.ppermute(send, "tensor", swap)

    half = slots * length // 2
    part = local_call(
        rank_body,
        shape(slots * length, 2 * rank),
        [SMEM, VMEM, VMEM, VMEM],
        flops=2 * slots * length * width * held * rank,
        moved=2 * slots * length * width,
    )(pick, arrived, down, up)
    both = lax.all_gather(part, "tensor", axis_index_groups=pairs)
    mine = lax.dynamic_slice_in_dim(both, core * half, half, axis=1)
    mine = mine.astype(f32).sum(0).astype(bf16).reshape(chips, half // chips, 2 * rank)
    pieces, came = lax.optimization_barrier((exchange(mine, "tensor", same_core), came))
    totals = local_call(
        total_body,
        shape(*mine.shape),
        [VMEM],
        moved=4 * half * 2 * rank,
    )(pieces)
    keep, give = local_call(
        pair_body,
        (shape(quarter, rows, out_block),) * 2,
        [VMEM, VMEM],
        moved=6 * chips * rows * out_block,
    )(after(own, totals), came)
    shared, keep, give = lax.optimization_barrier(
        (exchange(totals, "tensor", same_core), keep, give)
    )
    shared = shared.reshape(half, 2 * rank)
    ranks = lax.all_gather(shared, "tensor", axis_index_groups=pairs).reshape(part.shape)

    masked = pltpu.VMEM((slots * length, held * rank), bf16)
    contributions = local_call(
        expand_body,
        shape(slots, length, width),
        [SMEM, VMEM, VMEM, VMEM],
        [masked, masked],
        flops=2 * slots * length * width * held * rank,
        moved=2 * slots * length * width,
    )(pick, ranks, down, up)
    returned = exchange(contributions, "dp")

    keep, give, _ = lax.optimization_barrier((keep, give, contributions))
    far_other = lax.ppermute(after(far, give), "tensor", swap)
    near_other = lax.ppermute(after(near, give), "tensor", swap)
    crossed = lax.ppermute(give, "tensor", across)
    grad_down, grad_up = local_call(
        gradient_body,
        (shape(held, rank, block, dtype=f32), shape(held, rank, out_block, dtype=f32)),
        [SMEM, SMEM, VMEM, VMEM],
        [masked, masked],
        flops=2 * slots * length * width * held * rank,
        moved=2 * slots * length * width,
    )(pick, after(scale, give), ranks, arrived)
    base = local_call(
        base_body,
        shape(rows, block, dtype=f32),
        [SMEM, VMEM, VMEM, VMEM, VMEM, VMEM],
        flops=2 * rows * block * tensor_count * out_block,
        moved=2 * (2 * rows * tensor_count * out_block),
    )(after(place, give), near, near_other, far, far_other, weight)
    crossed, keep, base, grad_down, grad_up = lax.optimization_barrier(
        (crossed, keep, base, grad_down, grad_up)
    )
    summed = local_call(
        neighbour_body,
        (shape(rows, out_block),) * quarter,
        [VMEM, VMEM],
        moved=6 * quarter * rows * out_block,
    )(keep, crossed)
    parts = [summed[0], moved_along(summed[3], quarter)]
    parts += [moved_along(summed[1], 2), moved_along(summed[2], -2)]

    token_gradient, key_value_output = local_call(
        functools.partial(final_body, held),
        (shape(rows, block), shape(rows, out_block)),
        [SMEM, SMEM, SMEM, VMEM, VMEM] + [VMEM] * quarter,
        moved=2 * (3 * rows * block + slots * length * width),
    )(place, sequence_index, storage_row, base, returned, *parts)
    return (key_value_output, token_gradient, grad_down, grad_up)


def solution(mesh):
    in_specs = (
        P("dp", "tensor"),
        P("tensor", None),
        P("dp", None, "tensor"),
        P("dp", None, "tensor"),
        P("dp", "tensor"),
        P(),
        P(),
    )
    out_specs = (
        P("dp", "tensor"),
        P("dp", "tensor"),
        P("dp", None, "tensor"),
        P("dp", None, "tensor"),
    )
    return jax.shard_map(
        on_device, mesh=mesh, in_specs=in_specs, out_specs=out_specs, check_vma=False
    )
```
